256 devices in a mesh: inst: 32 (over z, x), tp: 8 (over y, core).
Axes of the slice: x: 4, y: 4, z: 8, core: 2. Of those that a mesh axis runs over, the one named last changes fastest.
Arguments:
- hidden: bfloat16 [64, 8192], P(None, 'inst'), may hold values from -400 to 400
- norm_gain: bfloat16 [8192], P('inst'), may hold values from 0.099609375 to 1.8984375
- w_query: bfloat16 [8192, 8192], P('inst', 'tp'), may hold values from -0.0625 to 0.0625
- w_key: bfloat16 [8192, 1024], P('inst', 'tp'), may hold values from -0.15625 to 0.15625
- w_value: bfloat16 [8192, 1024], P('inst', 'tp'), may hold values from -0.0625 to 0.0625
- w_out: bfloat16 [8192, 8192], P('tp', 'inst'), may hold values from -0.0625 to 0.0625
- kv_cache: bfloat16 [2, 1024, 256, 1024], P(None, 'inst', None, 'tp'), may hold values from -256 to 256
- lengths: int32 [32], replicated, may hold values from 1 to 8192, as said below
- slot_owner: int32 [1024], P('inst'), may hold values from -1 to 31, as said below
- slot_page: int32 [1024], P('inst'), may hold values from 0 to 31, as said below
Outputs:
- mixed: bfloat16 [64, 8192], P(None, 'inst')
The draws below stay inside these ranges and needn't reach their ends.
Inputs may be any that keep to these rules, and one draw needn't show every extreme that they name: `lengths`: A request holds ceil(length / 256) page slots; exactly one request has 32 full pages (length 8192). `slot_owner`: every request owns one or more slots; on each index of inst the live slots come first, and on some index all 32 slots are live and belong to one request. `slot_page`: the slots of one request hold its pages 0, 1, ... without gaps or repeats; empty slots hold 0.
All inputs are finite; a program needn't handle non-finite values.
Results may differ from the reference program's by a relative error of at most 0.0093.
Values may be sent and summed in bfloat16 or wider, within the bound.
A program may use at most 64 MiB of HBM per device.

```python
import math
import jax
import jax.numpy as jnp
from jax import lax

D = 8192
HQ = 64
KVH = 8
HD = 128
PAGE = 256
NEW = 2
SLOTS = 32
REQS = 32
TOKENS = 64
PAGES_ALL = 1024
N_INST = 32


def layout(key):
    seeds = jax.random.split(key, 6)
    donors = PAGES_ALL // SLOTS
    live_count = jax.random.randint(seeds[0], (donors,), SLOTS // 4, SLOTS // 2 + 1)
    full_donor = jax.random.randint(seeds[1], (), 0, donors)
    live_count = jnp.where(jnp.arange(donors) == full_donor, SLOTS, live_count)
    slot_ids = jnp.arange(PAGES_ALL, dtype=jnp.int32)
    used = slot_ids % SLOTS < live_count[slot_ids // SLOTS]
    on_full = slot_ids // SLOTS == full_donor
    others = used & jnp.logical_not(on_full)
    shuffle = jax.random.permutation(seeds[2], PAGES_ALL)
    ranked = (jnp.cumsum(others[shuffle].astype(jnp.int32)) - 1).astype(jnp.int32)
    rank_of = jnp.zeros((PAGES_ALL,), jnp.int32).at[shuffle].set(ranked)
    long_request = jax.random.randint(seeds[3], (), 0, REQS).astype(jnp.int32)
    spread_index = (rank_of % (REQS - 1)).astype(jnp.int32)
    spread_owner = spread_index + (spread_index >= long_request).astype(jnp.int32)
    owners = jnp.where(on_full, long_request, jnp.where(others, spread_owner, -1))
    member = (owners[None, :] == jnp.arange(REQS, dtype=jnp.int32)[:, None]).astype(jnp.int32)
    earlier = jnp.cumsum(member, axis=1) - member
    page_ids = jnp.sum(earlier * member, axis=0)
    counts = jnp.sum(member, axis=1)
    tails = jax.random.randint(seeds[5], (REQS,), 1, PAGE + 1)
    tails = jnp.where(jnp.arange(REQS, dtype=jnp.int32) == long_request, PAGE, tails)
    lengths = (counts - 1) * PAGE + tails
    return (lengths.astype(jnp.int32), owners.astype(jnp.int32), page_ids.astype(jnp.int32))


def draw_lengths(key, part):
    return layout(key)[0]


def draw_slot_owner(key, part):
    return layout(key)[1]


def draw_slot_page(key, part):
    return layout(key)[2]


def draw_hidden(key, part):
    key = jax.random.fold_in(key, 3)
    seeds = jax.random.split(key, 2)
    column = jnp.arange(D, dtype=jnp.float32) / D
    row_scale = jnp.exp(jax.random.uniform(seeds[1], (TOKENS, 1), jnp.float32, 0.0, math.log(10.0)))
    base = jnp.clip(jax.random.normal(seeds[0], (TOKENS, D), jnp.float32), -5.0, 5.0)
    rising = 3.0 ** column
    return (base * rising[None, :] * row_scale).astype(jnp.bfloat16)


def draw_kv_cache(key, part):
    key = jax.random.fold_in(key, 5)
    seeds = jax.random.split(key, 2)
    shape = (PAGES_ALL, PAGE, KVH, HD)
    keys_part = 2.0 * jnp.clip(jax.random.normal(seeds[0], shape, jnp.float32), -6.0, 6.0)
    values_part = jnp.clip(jax.random.normal(seeds[1], shape, jnp.float32), -6.0, 6.0)
    both = jnp.stack([keys_part, values_part]).reshape(2, PAGES_ALL, PAGE, KVH * HD)
    return both.astype(jnp.bfloat16)


def block_scale(stream_key, extent, cuts, least, top_value):
    loudness = 1.0
    for dim, parts in cuts:
        draws = jax.random.uniform(jax.random.fold_in(jax.random.fold_in(stream_key, 6), dim), (parts,), jnp.float32, least / len(cuts), top_value / len(cuts))
        loudness = loudness * jnp.repeat(jnp.exp(draws), extent[dim] // parts).reshape((-1,) + (1,) * (len(extent) - 1 - dim))
    return loudness


def normal_values(stream_key, extent, scale, limit, cuts=(), kind=jnp.bfloat16):
    result = scale * jax.random.normal(stream_key, extent, jnp.float32)
    if cuts:
        result = result * block_scale(stream_key, extent, cuts, -0.22, 0.18)
    return jnp.clip(result, -limit, limit).astype(kind)


def setup_inputs(seed: int = 0) -> dict:
    key_list = jax.random.split(jax.random.key(seed), 11)
    return {
        "hidden": draw_hidden(jax.random.fold_in(key_list[10], 71), 0),
        "norm_gain": jnp.clip(1.0 + 0.18 * jax.random.normal(key_list[1], (D,), jnp.float32), 0.099609375, 1.8984375).astype(jnp.bfloat16),
        "w_query": normal_values(key_list[2], (D, HQ * HD), D ** -0.5, 0.0625, ((0, 32), (1, 8))),
        "w_key": normal_values(key_list[3], (D, KVH * HD), (D // 6) ** -0.5, 0.15625, ((0, 32), (1, 8))),
        "w_value": normal_values(key_list[4], (D, KVH * HD), D ** -0.5, 0.0625, ((0, 32), (1, 8))),
        "w_out": normal_values(key_list[5], (HQ * HD, D), (HQ * HD) ** -0.5, 0.0625, ((0, 8), (1, 32))),
        "kv_cache": draw_kv_cache(jax.random.fold_in(key_list[10], 71), 0),
        "lengths": draw_lengths(jax.random.fold_in(key_list[10], 71), 0),
        "slot_owner": draw_slot_owner(jax.random.fold_in(key_list[10], 71), 0),
        "slot_page": draw_slot_page(jax.random.fold_in(key_list[10], 71), 0),
    }


NEG = -1e+30
EPS = 1e-05
THETA = 500000.0

def rotate(vector, positions, head_count):
    head_width = vector.shape[-1] // head_count
    halfway = head_width // 2
    inverse = THETA ** (-(jnp.arange(halfway, dtype=jnp.float32) * (2.0 / head_width)))
    angles = positions.astype(jnp.float32)[:, None] * inverse[None, :]
    cosine = jnp.cos(angles)[:, None, :]
    sine_part = jnp.sin(angles)[:, None, :]
    per_head = vector.reshape(vector.shape[0], head_count, head_width)
    first_half = per_head[..., :halfway]
    second_half = per_head[..., halfway:]
    turned = jnp.concatenate([first_half * cosine - second_half * sine_part, second_half * cosine + first_half * sine_part], axis=-1)
    return turned.reshape(vector.shape)

def block_terms(query_rows, keys_block, values_block, keep_mask, score_form, out_form):
    scores = jnp.einsum(score_form, query_rows.astype(jnp.float32), keys_block.astype(jnp.float32), precision=lax.Precision.HIGHEST) * HD ** (-0.5)
    scores = jnp.where(keep_mask, scores, NEG)
    top_score = lax.optimization_barrier(jnp.max(scores, axis=-1))
    weights = jnp.where(keep_mask, jnp.exp(scores - top_score[..., None]), 0.0)
    weight_sum = lax.optimization_barrier(jnp.sum(weights, axis=-1))
    rounded = weights.astype(jnp.bfloat16).astype(jnp.float32)
    output = jnp.einsum(out_form, rounded, values_block.astype(jnp.float32), precision=lax.Precision.HIGHEST)
    return (top_score, weight_sum, output)

def reference(hidden, norm_gain, w_query, w_key, w_value, w_out, kv_cache, lengths, slot_owner, slot_page):
    group_size = HQ // KVH
    floats = hidden.astype(jnp.float32)
    inverse = lax.rsqrt(lax.optimization_barrier(jnp.sum(floats * floats, axis=1)) / D + EPS)
    normed = (floats * norm_gain.astype(jnp.float32)[None, :]).astype(jnp.bfloat16)
    query_raw = jnp.dot(normed, w_query, preferred_element_type=jnp.float32) * inverse[:, None]
    key_raw = jnp.dot(normed, w_key, preferred_element_type=jnp.float32) * inverse[:, None]
    value_raw = jnp.dot(normed, w_value, preferred_element_type=jnp.float32) * inverse[:, None]
    positions = (lengths[:, None] + jnp.arange(NEW, dtype=jnp.int32)[None, :]).reshape(-1)
    queries = rotate(query_raw, positions, HQ).astype(jnp.bfloat16).reshape(REQS, NEW, KVH, group_size, HD)
    keys_new = rotate(key_raw, positions, KVH).astype(jnp.bfloat16).reshape(REQS, NEW, KVH, HD)
    values_new = value_raw.astype(jnp.bfloat16).reshape(REQS, NEW, KVH, HD)

    def donor_terms(donor_index):
        first_slot = donor_index * SLOTS
        owners = lax.dynamic_slice_in_dim(slot_owner, first_slot, SLOTS)
        page_ids = lax.dynamic_slice_in_dim(slot_page, first_slot, SLOTS)
        cache_block = lax.dynamic_slice_in_dim(kv_cache, first_slot, SLOTS, axis=1)
        owner_safe = jnp.maximum(owners, 0)
        query_rows = queries[owner_safe]
        offsets = page_ids[:, None] * PAGE + jnp.arange(PAGE, dtype=jnp.int32)[None, :]
        valid_mask = (owners[:, None] >= 0) & (offsets < lengths[owner_safe][:, None])
        keys_block = cache_block[0].reshape(SLOTS, PAGE, KVH, HD)
        values_block = cache_block[1].reshape(SLOTS, PAGE, KVH, HD)
        return block_terms(query_rows, keys_block, values_block, valid_mask[:, None, None, None, :], 'stkgd,spkd->stkgp', 'stkgp,spkd->stkgd')
    tops, weight_sums, outputs = lax.map(donor_terms, jnp.arange(N_INST, dtype=jnp.int32))
    flat_width = NEW * HQ
    tops = tops.reshape(PAGES_ALL, flat_width)
    weight_sums = weight_sums.reshape(PAGES_ALL, flat_width)
    outputs = outputs.reshape(PAGES_ALL, flat_width, HD)
    causal = jnp.arange(NEW)[None, :] <= jnp.arange(NEW)[:, None]
    fresh_top, fresh_sum, fresh_out = block_terms(queries, keys_new, values_new, causal[None, :, None, None, :], 'ntkgd,nukd->ntkgu', 'ntkgu,nukd->ntkgd')
    fresh_top = fresh_top.reshape(REQS, flat_width)
    fresh_sum = fresh_sum.reshape(REQS, flat_width)
    fresh_out = fresh_out.reshape(REQS, flat_width, HD)
    owner_index = jnp.where(slot_owner < 0, REQS, slot_owner)
    top_req = jnp.full((REQS + 1, flat_width), NEG, jnp.float32).at[owner_index].max(tops)
    peak_score = jnp.maximum(top_req[:REQS], fresh_top)
    peak_ext = jnp.concatenate([peak_score, jnp.full((1, flat_width), NEG, jnp.float32)], axis=0)
    factor = jnp.exp(tops - peak_ext[owner_index])
    fresh_factor = jnp.exp(fresh_top - peak_score)
    total = jnp.zeros((REQS + 1, flat_width), jnp.float32).at[owner_index].add(factor * weight_sums)[:REQS] + fresh_factor * fresh_sum
    combined = jnp.zeros((REQS + 1, flat_width, HD), jnp.float32).at[owner_index].add(factor[..., None] * outputs)[:REQS] + fresh_factor[..., None] * fresh_out
    attention = (combined / total[..., None]).astype(jnp.bfloat16).reshape(TOKENS, HQ * HD)
    return jnp.dot(attention, w_out, preferred_element_type=jnp.float32).astype(jnp.bfloat16)
```

```python
import functools

import jax
import jax.numpy as jnp
from jax import lax
from jax.experimental import pallas as pl
from jax.experimental.pallas import tpu as pltpu
from jax.sharding import PartitionSpec as P

D = 8192
HD = 128
NEG = -1e30
EPS = 1e-05
THETA = 500000.0
SCALE = HD ** -0.5
N_INST = 32
N_TP = 8
OWNERS = 16
MESH = pl.DeviceIdType.MESH
F32 = jnp.float32
BF16 = jnp.bfloat16


def iota(shape, dim):
    return lax.broadcasted_iota(jnp.int32, shape, dim)


def far_first(k):
    kz, kx = k // 4, k % 4
    dz = lax.rem(4 + (1 - 2 * lax.rem(kz, 2)) * ((kz + 1) // 2), 8)
    dx = lax.rem(2 + (1 - 2 * lax.rem(kx, 2)) * ((kx + 1) // 2), 4)
    return dz, dx


def rope(rows, cosine, sine):
    return rows * cosine + pltpu.roll(rows, 64, 1) * sine


def kernel(
    hid_hbm, gain_ref, wq_hbm, wk_hbm, wv_hbm, wo_hbm, kv_hbm, len_hbm, own_hbm, page_hbm,
    out_ref,
    hid, hid32, wq, wkv, wo, keys, vals, lens, owns, pages,
    q_src, q_rcv, kv_src, kv_rcv, sq_src, sq_rcv, q_all, kv_new,
    sel, sel_t, bias, ownv, acc_src, acc_rcv, st_src, st_rcv, att_all, tp_all,
    local_sem, send_sem, recv_sem,
):
    inst = lax.axis_index("inst")
    tp = lax.axis_index("tp")
    z, x = inst // 4, lax.rem(inst, 4)
    is_owner = z < 4

    def local(i, src, dst):
        return pltpu.make_async_copy(src, dst, local_sem.at[i])

    loads = [
        local(0, hid_hbm, hid),
        local(1, wq_hbm, wq),
        local(2, wk_hbm, wkv.at[:, :HD]),
        local(3, wv_hbm, wkv.at[:, HD:]),
        local(4, own_hbm, owns),
        local(5, page_hbm, pages),
        local(6, len_hbm, lens),
        local(7, kv_hbm.at[0], keys),
        local(8, kv_hbm.at[1], vals),
        local(9, wo_hbm, wo),
    ]
    barrier = pltpu.get_barrier_semaphore()

    @pl.when(is_owner)
    def _():
        @pl.loop(1, N_INST)
        def _(k):
            to = lax.rem(inst + k, N_INST)
            pl.semaphore_signal(barrier, inc=1, device_id={"inst": to}, device_id_type=MESH)

    @pl.loop(1, N_TP)
    def _(k):
        to = lax.rem(tp + k, N_TP)
        pl.semaphore_signal(barrier, inc=1, device_id={"tp": to}, device_id_type=MESH)

    for load in loads:
        load.start()

    def remote(src, dst, i, to):
        return pltpu.make_async_remote_copy(
            src_ref=src, dst_ref=dst, send_sem=send_sem.at[i], recv_sem=recv_sem.at[i],
            device_id=to, device_id_type=MESH,
        )

    def arrived(ref, i):
        pltpu.make_async_copy(ref, ref, recv_sem.at[i]).wait()

    def departed(ref, i):
        pltpu.make_async_copy(ref, ref, send_sem.at[i]).wait()

    def place(owner):
        return lax.rem(inst - owner - 1 + 2 * N_INST, N_INST)

    def to_owners(send):
        @pl.loop(0, OWNERS)
        def _(k):
            zo = lax.rem(k, 4)
            xo = lax.rem(x + far_first(k // 4)[1], 4)
            owner = zo * 4 + xo

            @pl.when(owner != inst)
            def _():
                send(owner)

    def to_all(src, dst, i):
        @pl.loop(0, N_INST - 1)
        def _(k):
            dz, dx = far_first(k)
            to = lax.rem(z + dz, 8) * 4 + lax.rem(x + dx, 4)
            remote(src, dst, i, {"inst": to}).start()

    loads[0].wait()
    for c in range(2):
        hid32[c] = hid[:, HD * c : HD * c + HD].astype(F32)
    rows = jnp.concatenate(
        [
            jnp.concatenate(
                [hid32[c, pl.ds(16 * g + t, 8, stride=2), :] for g in range(4) for t in range(2)], axis=0
            )
            for c in range(2)
        ],
        axis=1,
    )
    squares = jnp.sum(rows * rows, axis=1, keepdims=True)
    spread = jnp.where(iota((64, HD), 0) == iota((64, HD), 1), squares, 0.0)
    sq_src[...] = jnp.sum(spread, axis=0, keepdims=True)
    normed = (rows * gain_ref[...].astype(F32)).astype(BF16)
    loads[1].wait()
    raw = jnp.dot(normed, wq[...], preferred_element_type=F32).astype(BF16)
    for owner in range(OWNERS):
        zo, g = owner // 4, owner % 4
        for k in range(2):
            h = 2 * zo + k
            q_src[owner, 16 * k : 16 * k + 16, :] = raw[16 * g : 16 * g + 16, HD * h : HD * h + HD]
    loads[2].wait()
    loads[3].wait()
    raw = jnp.dot(normed, wkv[...], preferred_element_type=F32).astype(BF16)
    for g in range(4):
        for k in range(2):
            kv_src[g, 16 * k : 16 * k + 16, :] = raw[16 * g : 16 * g + 16, HD * k : HD * k + HD]

    pl.semaphore_wait(barrier, OWNERS + N_TP - 1 - is_owner.astype(jnp.int32))

    def send_query(owner):
        remote(sq_src, sq_rcv.at[place(owner)], 0, {"inst": owner}).start()
        remote(q_src.at[owner], q_rcv.at[place(owner)], 1, {"inst": owner}).start()

    to_owners(send_query)
    for g in range(4):

        @pl.when(inst != g)
        def _():
            remote(kv_src.at[g], kv_rcv.at[place(g)], 2, {"inst": g}).start()

    loads[4].wait()
    loads[5].wait()
    loads[6].wait()
    shifted = iota((16, 512), 1)
    row = iota((16, 512), 0)
    shifted = shifted - ((row // 4) * 128 + (lax.rem(row, 4) // 2) * 16 + lax.rem(row, 2) * 8)

    @pl.loop(0, 32)
    def _(s):
        owner = owns[s]
        safe = jnp.maximum(owner, 0)
        target = jnp.where(owner >= 0, (safe // 8) * 32 + lax.rem(safe, 8), -1000)
        limit = lens[safe] - pages[s] * 256
        sel[pl.ds(pl.multiple_of(16 * s, 16), 16), :] = (shifted == target).astype(F32).astype(BF16)
        bias[pl.ds(s, 1), :] = jnp.where(iota((1, 256), 1) < limit, 0.0, NEG)
        ownv[pl.ds(s, 1), :] = jnp.full((1, HD), owner, jnp.int32)

    sel_t[...] = sel[...].astype(F32).T.astype(BF16)

    @pl.when(is_owner)
    def _():
        spot = iota((16, HD), 0)
        position = jnp.zeros((16, HD), jnp.int32)
        for k in range(8):
            position = jnp.where(lax.rem(spot, 8) == k, lens[8 * x + k], position)
        position = position + spot // 8
        lane = iota((16, HD), 1)
        index = lax.rem(lane, 64).astype(F32)
        angle = position.astype(F32) * jnp.exp(index * (-2.0 / HD * 13.122363377404328))
        cosine = jnp.cos(angle)
        sine = jnp.sin(angle) * jnp.where(lane < 64, -1.0, 1.0)
        arrived(sq_rcv, 0)
        total = jnp.sum(sq_rcv[...], axis=0) + sq_src[...]
        mine = jnp.where(lane == 16 * x + spot, total, 0.0)
        inverse = lax.rsqrt(jnp.sum(mine, axis=1, keepdims=True) / D + EPS)
        arrived(q_rcv, 1)
        joined = jnp.sum(q_rcv[...].astype(F32), axis=0) + q_src[inst].astype(F32)
        for k in range(2):
            part = rope(joined[16 * k : 16 * k + 16] * inverse, cosine, sine)
            q_all[inst, 16 * k : 16 * k + 16, :] = part.astype(BF16)
        to_all(q_all.at[inst], q_all.at[inst], 3)

        @pl.when(z == 0)
        def _():
            arrived(kv_rcv, 2)
            both = jnp.sum(kv_rcv[...].astype(F32), axis=0) + kv_src[inst].astype(F32)
            both = both * jnp.concatenate([inverse, inverse], axis=0)
            kv_new[0:16, :] = rope(both[0:16], cosine, sine).astype(BF16)
            kv_new[16:32, :] = both[16:32].astype(BF16)
            for k in range(1, 4):
                remote(kv_new, kv_new, 4, {"inst": 4 * k + x}).start()

    loads[7].wait()
    loads[8].wait()

    @pl.when(is_owner)
    def _():
        arrived(q_all.at[0:15], 3)

    @pl.when(jnp.logical_not(is_owner))
    def _():
        arrived(q_all, 3)

    queries = jnp.dot(sel[...], q_all[...].reshape(512, HD), preferred_element_type=F32).astype(BF16)
    scores = lax.dot_general(
        queries.reshape(32, 16, HD), keys[...], (((2,), (2,)), ((0,), (0,))), preferred_element_type=F32
    )
    scores = scores * SCALE + bias[...][:, None, :]
    top = jnp.max(scores, axis=2, keepdims=True)
    weights = jnp.exp(scores - top)
    weight_sum = jnp.sum(weights, axis=2, keepdims=True)
    part = lax.dot_general(
        weights.astype(BF16), vals[...], (((2,), (1,)), ((0,), (0,))), preferred_element_type=F32
    )
    diagonal = iota((32, 16, HD), 1) == iota((32, 16, HD), 2)
    top_row = jnp.sum(jnp.where(diagonal, top, 0.0), axis=1)
    sum_row = jnp.sum(jnp.where(diagonal, weight_sum, 0.0), axis=1)
    owner_row = ownv[...]
    same = owner_row[:, None, :] == owner_row[None, :, :]
    peak_row = jnp.max(jnp.where(same, top_row[None, :, :], NEG), axis=1)
    factor = jnp.exp(top_row - peak_row)
    factor_col = jnp.sum(jnp.where(diagonal, factor[:, None, :], 0.0), axis=2, keepdims=True)
    part = (part * factor_col).reshape(512, HD)
    high = part.astype(BF16)
    low = (part - high.astype(F32)).astype(BF16)
    both = jnp.dot(sel_t[...], jnp.concatenate([high, low], axis=1), preferred_element_type=F32)
    acc_src[...] = (both[:, :HD] + both[:, HD:]).astype(BF16).reshape(OWNERS, 32, HD)
    member = owner_row[None, :, :] == iota((32, 32, HD), 0)
    top_req = jnp.max(jnp.where(member, top_row[None, :, :], NEG), axis=1)
    sum_req = jnp.sum(jnp.where(member, (factor * sum_row)[None, :, :], 0.0), axis=1)
    st_src[...] = jnp.where(
        iota((32, HD), 1) < 16, top_req, pltpu.roll(sum_req, 16, 1)
    ).reshape(4, 8, HD)

    def send_parts(owner):
        remote(st_src.at[lax.rem(owner, 4)], st_rcv.at[place(owner)], 5, {"inst": owner}).start()
        remote(acc_src.at[owner], acc_rcv.at[place(owner)], 6, {"inst": owner}).start()

    to_owners(send_parts)

    @pl.when(is_owner)
    def _():
        @pl.when(z > 0)
        def _():
            arrived(kv_new, 4)

        row = iota((32, 16), 0)
        key = iota((32, 16), 1)
        seen = (lax.rem(row, 8) == lax.rem(key, 8)) & (key // 8 <= lax.rem(row, 16) // 8)
        fresh = lax.dot_general(
            q_all[inst], kv_new[0:16, :], (((1,), (1,)), ((), ())), preferred_element_type=F32
        ) * SCALE
        fresh = jnp.where(seen, fresh, NEG)
        fresh_top = jnp.max(fresh, axis=1, keepdims=True)
        weights = jnp.where(seen, jnp.exp(fresh - fresh_top), 0.0)
        fresh_sum = jnp.sum(weights, axis=1, keepdims=True)
        fresh_out = jnp.dot(weights.astype(BF16), kv_new[16:32, :], preferred_element_type=F32)
        lane = iota((8, HD), 1)
        top_lanes = jnp.full((8, HD), NEG, F32)
        sum_lanes = jnp.zeros((8, HD), F32)
        for k in range(4):
            top_lanes = jnp.where(lane == k, fresh_top[8 * k : 8 * k + 8], top_lanes)
            sum_lanes = jnp.where(lane == k, fresh_sum[8 * k : 8 * k + 8], sum_lanes)

        arrived(st_rcv, 5)
        stats = jnp.concatenate([st_rcv[...], st_src[pl.ds(x, 1)]], axis=0).reshape(256, HD)
        tops = pltpu.roll(stats, lax.rem(HD - 4 * z, HD), 1)
        sums = pltpu.roll(tops, HD - 16, 1).reshape(32, 8, HD)
        tops = tops.reshape(32, 8, HD)
        peak = jnp.maximum(jnp.max(tops, axis=0), top_lanes)
        scale = jnp.exp(tops - peak[None])
        fresh_scale = jnp.exp(top_lanes - peak)
        total = jnp.sum(scale * sums, axis=0) + fresh_scale * sum_lanes
        arrived(acc_rcv, 6)
        parts = jnp.concatenate([acc_rcv[...], acc_src[pl.ds(inst, 1)]], axis=0).astype(F32)
        done = []
        for k in range(4):
            out = jnp.sum(parts[:, 8 * k : 8 * k + 8, :] * scale[:, :, k : k + 1], axis=0)
            out = out + fresh_scale[:, k : k + 1] * fresh_out[8 * k : 8 * k + 8]
            done.append(out / total[:, k : k + 1])
        att_all[inst] = jnp.concatenate(done, axis=0).astype(BF16)
        to_all(att_all.at[inst], att_all.at[inst], 7)

    loads[9].wait()

    @pl.when(is_owner)
    def _():
        arrived(att_all.at[0:15], 7)

    @pl.when(jnp.logical_not(is_owner))
    def _():
        arrived(att_all, 7)

    attention = jnp.concatenate(
        [
            jnp.concatenate(
                [att_all[4 * zo + g, 16 * k : 16 * k + 16, :] for zo in range(4) for k in range(2)], axis=1
            )
            for g in range(4)
        ],
        axis=0,
    )
    tp_all[tp] = jnp.dot(attention, wo[...], preferred_element_type=F32).astype(BF16)

    @pl.loop(1, N_TP)
    def _(k):
        to = lax.rem(tp + k, N_TP)
        remote(tp_all.at[tp], tp_all.at[tp], 8, {"tp": to}).start()

    arrived(tp_all.at[0:7], 8)
    mixed = tp_all[0].astype(F32)
    for k in range(1, N_TP):
        mixed = mixed + tp_all[k].astype(F32)
    for g in range(4):
        for t in range(2):
            first = 16 * g + 8 * t
            for c in range(2):
                cols = slice(HD * c, HD * c + HD)
                out_ref[c, pl.ds(16 * g + t, 8, stride=2), :] = mixed[first : first + 8, cols]

    departed(tp_all.at[0:7], 8)

    @pl.when(is_owner)
    def _():
        for i, ref in ((1, q_src), (6, acc_src)):
            departed(ref.at[0:15], i)
        departed(sq_rcv.at[0:15], 0)
        departed(st_rcv.at[0:15], 5)
        departed(q_rcv, 3)
        departed(acc_rcv, 7)

        @pl.when(z == 0)
        def _():
            departed(kv_src.at[0:3], 2)
            departed(kv_src.at[0:3], 4)

        @pl.when(z > 0)
        def _():
            departed(kv_src, 2)

    @pl.when(jnp.logical_not(is_owner))
    def _():
        for i, ref in ((1, q_src), (6, acc_src), (2, kv_src)):
            departed(ref, i)
        departed(sq_rcv.at[0:16], 0)
        departed(st_rcv.at[0:16], 5)


def on_device(
    hidden, norm_gain, w_query, w_key, w_value, w_out, kv_cache, lengths, slot_owner, slot_page
):
    hbm = pl.BlockSpec(memory_space=pl.ANY)
    vmem = pl.BlockSpec(memory_space=pltpu.VMEM)
    mixed = pl.pallas_call(
        kernel,
        out_shape=jax.ShapeDtypeStruct((2, 64, HD), F32),
        in_specs=[hbm, vmem] + [hbm] * 8,
        out_specs=vmem,
        scratch_shapes=[
            pltpu.VMEM((64, 256), BF16),
            pltpu.VMEM((2, 64, HD), F32),
            pltpu.VMEM((256, 1024), BF16),
            pltpu.VMEM((256, 256), BF16),
            pltpu.VMEM((1024, 256), BF16),
            pltpu.VMEM((32, 256, HD), BF16),
            pltpu.VMEM((32, 256, HD), BF16),
            pltpu.SMEM((32,), jnp.int32),
            pltpu.SMEM((32,), jnp.int32),
            pltpu.SMEM((32,), jnp.int32),
            pltpu.VMEM((OWNERS, 32, HD), BF16),
            pltpu.VMEM((31, 32, HD), BF16),
            pltpu.VMEM((4, 32, HD), BF16),
            pltpu.VMEM((31, 32, HD), BF16),
            pltpu.VMEM((1, HD), F32),
            pltpu.VMEM((31, 1, HD), F32),
            pltpu.VMEM((OWNERS, 32, HD), BF16),
            pltpu.VMEM((32, HD), BF16),
            pltpu.VMEM((512, 512), BF16),
            pltpu.VMEM((512, 512), BF16),
            pltpu.VMEM((32, 256), F32),
            pltpu.VMEM((32, HD), jnp.int32),
            pltpu.VMEM((OWNERS, 32, HD), BF16),
            pltpu.VMEM((31, 32, HD), BF16),
            pltpu.VMEM((4, 8, HD), F32),
            pltpu.VMEM((31, 8, HD), F32),
            pltpu.VMEM((OWNERS, 32, HD), BF16),
            pltpu.VMEM((N_TP, 64, 256), BF16),
            pltpu.SemaphoreType.DMA((10,)),
            pltpu.SemaphoreType.DMA((9,)),
            pltpu.SemaphoreType.DMA((9,)),
        ],
        compiler_params=pltpu.CompilerParams(
            collective_id=0, has_side_effects=True, vmem_limit_bytes=40 * 1024 * 1024
        ),
        name="paged_attention",
    )(
        hidden, norm_gain.reshape(1, -1), w_query, w_key, w_value, w_out, kv_cache,
        lengths, slot_owner, slot_page,
    )
    return mixed.transpose(1, 0, 2).reshape(64, 256).astype(BF16)


def solution(mesh):
    return jax.shard_map(
        on_device,
        mesh=mesh,
        in_specs=(
            P(None, "inst"),
            P("inst"),
            P("inst", "tp"),
            P("inst", "tp"),
            P("inst", "tp"),
            P("tp", "inst"),
            P(None, "inst", None, "tp"),
            P(),
            P("inst"),
            P("inst"),
        ),
        out_specs=P(None, "inst"),
        check_vma=False,
    )
```

```python
import functools

import jax
import jax.numpy as jnp
from jax import lax
from jax.experimental import pallas as pl
from jax.experimental.pallas import tpu as pltpu
from jax.sharding import PartitionSpec as P

D = 8192
HD = 128
NEG = -1e30
EPS = 1e-05
THETA = 500000.0
SCALE = HD ** -0.5
N_INST = 32
N_TP = 8
MESH = pl.DeviceIdType.MESH
F32 = jnp.float32
BF16 = jnp.bfloat16


def iota(shape, dim):
    return lax.broadcasted_iota(jnp.int32, shape, dim)


def far_first():
    offsets = [(dz, dx) for dz in range(8) for dx in range(4) if dz or dx]
    return sorted(offsets, key=lambda o: -min(o[0], 8 - o[0]) - min(o[1], 4 - o[1]))


def rope(rows, cosine, sine):
    return rows * cosine + pltpu.roll(rows, 64, 1) * sine


def kernel(
    hid_hbm, gain_hbm, wq_hbm, wk_hbm, wv_hbm, wo_hbm, kv_hbm, len_hbm, own_hbm, page_hbm,
    out_ref,
    hid, hid32, gain, wq, wkv, wo, keys, vals, lens, owns, pages,
    q_src, q_rcv, kv_src, kv_rcv, sq_src, sq_rcv, q_all, kv_new,
    sel, sel_t, bias, member, acc_src, acc_rcv, st_src, st_rcv, att_all, tp_all,
    local_sem, send_sem, recv_sem,
):
    inst = lax.axis_index("inst")
    tp = lax.axis_index("tp")
    z, x = inst // 4, lax.rem(inst, 4)
    peers = [
        lax.rem(z + dz, 8) * 4 + lax.rem(x + dx, 4) for dz, dx in far_first()
    ]
    tp_peers = [lax.rem(tp + k, N_TP) for k in (4, 5, 3, 2, 6, 1, 7)]

    def local(i, src, dst):
        return pltpu.make_async_copy(src, dst, local_sem.at[i])

    loads = [
        local(0, hid_hbm, hid),
        local(1, wq_hbm, wq),
        local(2, wk_hbm, wkv.at[:, :HD]),
        local(3, wv_hbm, wkv.at[:, HD:]),
        local(4, own_hbm, owns),
        local(5, page_hbm, pages),
        local(6, len_hbm, lens),
        local(7, kv_hbm.at[0], keys),
        local(8, kv_hbm.at[1], vals),
        local(9, wo_hbm, wo),
        local(10, gain_hbm, gain),
    ]
    barrier = pltpu.get_barrier_semaphore()
    for to in peers:
        pl.semaphore_signal(barrier, inc=1, device_id={"inst": to}, device_id_type=MESH)
    for to in tp_peers:
        pl.semaphore_signal(barrier, inc=1, device_id={"tp": to}, device_id_type=MESH)
    for load in [loads[0], loads[10]] + loads[1:10]:
        load.start()

    def remote(src, dst, i, to):
        return pltpu.make_async_remote_copy(
            src_ref=src, dst_ref=dst, send_sem=send_sem.at[i], recv_sem=recv_sem.at[i],
            device_id=to, device_id_type=MESH,
        )

    def arrived(ref, i):
        pltpu.make_async_copy(ref, ref, recv_sem.at[i]).wait()

    def departed(ref, i):
        pltpu.make_async_copy(ref, ref, send_sem.at[i]).wait()

    def drain(stage):
        if stage > 0:
            departed(sq_rcv, 0)
            departed(q_rcv, 1)

            @pl.when(z == 0)
            def _():
                departed(kv_src.at[0:3], 2)

            @pl.when(z > 0)
            def _():
                departed(kv_src, 2)

        if stage > 1:
            departed(q_rcv, 3)

            @pl.when(z == 0)
            def _():
                departed(kv_rcv.at[0:7], 4)

        if stage > 2:
            departed(st_rcv, 5)
            departed(acc_rcv, 6)
        if stage > 3:
            departed(acc_rcv, 7)
            departed(tp_all.at[0:7], 8)

    def place(to):
        return lax.rem(inst - to + (N_INST - 1), N_INST)

    places = [place(to) for to in peers]

    def to_all(src, dst, i):
        for to in peers:
            remote(src, dst, i, {"inst": to}).start()

    loads[0].wait()
    for c in range(2):
        hid32[c] = hid[:, HD * c : HD * c + HD].astype(F32)
    rows = jnp.concatenate(
        [
            jnp.concatenate(
                [hid32[c, pl.ds(16 * g + t, 8, stride=2), :] for g in range(4) for t in range(2)], axis=0
            )
            for c in range(2)
        ],
        axis=1,
    )
    squares = jnp.sum(rows * rows, axis=1, keepdims=True)
    spread = jnp.where(iota((64, HD), 0) == iota((64, HD), 1), squares, 0.0)
    sq_src[...] = jnp.sum(spread, axis=0, keepdims=True)
    loads[10].wait()
    normed = (rows * gain[...].astype(F32).reshape(1, 256)).astype(BF16)
    loads[1].wait()
    raw = jnp.dot(normed, wq[...], preferred_element_type=F32).astype(BF16)
    for h in range(8):
        for g in range(4):
            q_src[4 * h + g] = raw[16 * g : 16 * g + 16, HD * h : HD * h + HD]
    loads[2].wait()
    loads[3].wait()
    raw = jnp.dot(normed, wkv[...], preferred_element_type=F32).astype(BF16)
    for g in range(4):
        for k in range(2):
            kv_src[g, 16 * k : 16 * k + 16, :] = raw[16 * g : 16 * g + 16, HD * k : HD * k + HD]

    pl.semaphore_wait(barrier, N_INST - 1 + N_TP - 1)

    for to, there in zip(peers, places):
        remote(q_src.at[to], q_rcv.at[there], 1, {"inst": to}).start()
        remote(sq_src, sq_rcv.at[there], 0, {"inst": to}).start()
    for g in range(4):

        @pl.when(inst != g)
        def _():
            remote(kv_src.at[g], kv_rcv.at[place(g)], 2, {"inst": g}).start()

    loads[6].wait()
    spot = iota((16, HD), 0)
    lane = iota((16, HD), 1)
    position = jnp.zeros((16, HD), jnp.int32)
    for k in range(8):
        position = jnp.where(lax.rem(spot, 8) == k, lens[8 * x + k], position)
    position = position + spot // 8
    index = lax.rem(lane, 64).astype(F32)
    angle = position.astype(F32) * jnp.exp(index * (-2.0 / HD * 13.122363377404328))
    cosine = jnp.cos(angle)
    sine = jnp.sin(angle) * jnp.where(lane < 64, -1.0, 1.0)

    arrived(sq_rcv, 0)
    total = jnp.sum(sq_rcv[...], axis=0) + sq_src[...]
    mine = jnp.where(lane == 16 * x + spot, total, 0.0)
    inverse = lax.rsqrt(jnp.sum(mine, axis=1, keepdims=True) / D + EPS)
    arrived(q_rcv, 1)
    joined = jnp.sum(q_rcv[...].astype(F32), axis=0) + q_src[inst].astype(F32)
    q_all[inst] = rope(joined * inverse, cosine, sine).astype(BF16)
    to_all(q_all.at[inst], q_all.at[inst], 3)

    loads[4].wait()
    loads[5].wait()
    row = iota((16, 512), 0)
    shifted = iota((16, 512), 1) - ((row // 2) * 64 + lax.rem(row, 2) * 8)
    column = iota((1, 512), 1)

    def slot(s, targets):
        owner = owns[s]
        safe = jnp.maximum(owner, 0)
        target = jnp.where(owner >= 0, (safe // 8) * 16 + lax.rem(safe, 8), -1000)
        limit = jnp.where(owner >= 0, lens[safe] - pages[s] * 256, 0)
        sel[pl.ds(pl.multiple_of(16 * s, 16), 16), :] = (shifted == target).astype(F32).astype(BF16)
        bias[s] = jnp.where(iota((1, 256), 1) < limit, 0.0, NEG)
        member[s] = (iota((1, HD), 1) == owner).astype(jnp.int32)
        return jnp.where(column // 16 == s, target, targets)

    targets = lax.fori_loop(0, 32, slot, jnp.zeros((1, 512), jnp.int32), unroll=4)
    j = lax.rem(column, 16)
    targets = targets + (j // 2) * 64 + lax.rem(j, 2) * 8
    sel_t[...] = (iota((512, 512), 0) == targets).astype(F32).astype(BF16)

    @pl.when(z == 0)
    def _():
        arrived(kv_rcv, 2)
        both = jnp.sum(kv_rcv[...].astype(F32), axis=0) + kv_src[inst].astype(F32)
        both = both * jnp.concatenate([inverse, inverse], axis=0)
        kv_new[0:16, :] = rope(both[0:16], cosine, sine).astype(BF16)
        kv_new[16:32, :] = both[16:32].astype(BF16)
        for k in range(1, 8):
            remote(kv_new, kv_new, 4, {"inst": 4 * k + x}).start()

    loads[7].wait()
    loads[8].wait()
    arrived(q_all.at[0:31], 3)
    queries = jnp.dot(sel[...], q_all[...].reshape(512, HD), preferred_element_type=F32).astype(BF16)
    scores = lax.dot_general(
        queries.reshape(32, 16, HD), keys[...], (((2,), (2,)), ((0,), (0,))), preferred_element_type=F32
    )
    scores = scores * SCALE + bias[...]
    top = jnp.max(scores, axis=2, keepdims=True)
    weights = jnp.exp(scores - top)
    weight_sum = jnp.sum(weights, axis=2, keepdims=True)
    part = lax.dot_general(
        weights.astype(BF16), vals[...], (((2,), (1,)), ((0,), (0,))), preferred_element_type=F32
    )
    belongs = member[...] > 0
    top_req = jnp.max(jnp.where(belongs, top, NEG), axis=0)
    peak = jnp.max(jnp.where(belongs, top_req[None], NEG), axis=2, keepdims=True)
    factor = jnp.exp(top - peak)
    sum_req = jnp.sum(jnp.where(belongs, factor * weight_sum, 0.0), axis=0)
    stats = jnp.where(iota((16, HD), 1) < 32, top_req, pltpu.roll(sum_req, 32, 1))
    st_src[...] = stats.reshape(8, 2, HD)
    part = (part * factor).reshape(512, HD)
    high = part.astype(BF16)
    low = (part - high.astype(F32)).astype(BF16)
    both = jnp.dot(sel_t[...], jnp.concatenate([high, low], axis=1), preferred_element_type=F32)
    acc_src[...] = (both[:, :HD] + both[:, HD:]).astype(BF16).reshape(N_INST, 16, HD)

    for to, there in zip(peers, places):
        remote(acc_src.at[to], acc_rcv.at[there], 6, {"inst": to}).start()
        remote(st_src.at[to // 4], st_rcv.at[there], 5, {"inst": to}).start()

    @pl.when(z > 0)
    def _():
        arrived(kv_new, 4)

    row = iota((16, 16), 0)
    key = iota((16, 16), 1)
    seen = (lax.rem(row, 8) == lax.rem(key, 8)) & (key // 8 <= row // 8)
    fresh = lax.dot_general(
        q_all[inst], kv_new[0:16, :], (((1,), (1,)), ((), ())), preferred_element_type=F32
    ) * SCALE
    fresh = jnp.where(seen, fresh, NEG)
    fresh_top = jnp.max(fresh, axis=1, keepdims=True)
    weights = jnp.where(seen, jnp.exp(fresh - fresh_top), 0.0)
    fresh_sum = jnp.sum(weights, axis=1, keepdims=True)
    fresh_out = jnp.dot(weights.astype(BF16), kv_new[16:32, :], preferred_element_type=F32)

    arrived(st_rcv, 5)
    own = st_src[pl.ds(z, 1)]
    stats = jnp.concatenate(
        [st_rcv[:, 0, :], own[:, 0, :], st_rcv[:, 1, :], own[:, 1, :]], axis=0
    )
    stats = pltpu.roll(stats, lax.rem(HD - 8 * x, HD), 1).T
    tops, sums = stats[0:8], stats[32:40]
    scales, fresh_scales, totals = [], [], []
    for t in range(2):
        first = fresh_top[8 * t : 8 * t + 8]
        held = tops[:, 32 * t : 32 * t + 32]
        peak = jnp.maximum(jnp.max(held, axis=1, keepdims=True), first)
        scale = jnp.exp(held - peak)
        fresh_scale = jnp.exp(first - peak)
        total = jnp.sum(scale * sums[:, 32 * t : 32 * t + 32], axis=1, keepdims=True)
        totals.append(total + fresh_scale * fresh_sum[8 * t : 8 * t + 8])
        scales.append(scale)
        fresh_scales.append(fresh_scale)
    scale = jnp.concatenate(scales, axis=0)
    arrived(acc_rcv, 6)
    out = jnp.concatenate(fresh_scales, axis=0) * fresh_out
    for d in range(N_INST):
        held = acc_rcv[d] if d < N_INST - 1 else acc_src[inst]
        out = out + scale[:, d : d + 1] * held.astype(F32)
    att_all[inst] = (out / jnp.concatenate(totals, axis=0)).astype(BF16)
    to_all(att_all.at[inst], att_all.at[inst], 7)

    loads[9].wait()
    arrived(att_all.at[0:31], 7)
    attention = jnp.concatenate(
        [jnp.concatenate([att_all[4 * h + g] for h in range(8)], axis=1) for g in range(4)], axis=0
    )
    tp_all[tp] = jnp.dot(attention, wo[...], preferred_element_type=F32).astype(BF16)
    for to in tp_peers:
        remote(tp_all.at[tp], tp_all.at[tp], 8, {"tp": to}).start()
    arrived(tp_all.at[0:7], 8)
    mixed = tp_all[0].astype(F32)
    for k in range(1, N_TP):
        mixed = mixed + tp_all[k].astype(F32)
    for g in range(4):
        for t in range(2):
            first = 16 * g + 8 * t
            for c in range(2):
                cols = slice(HD * c, HD * c + HD)
                out_ref[c, pl.ds(16 * g + t, 8, stride=2), :] = mixed[first : first + 8, cols]

    drain(4)


def on_device(
    hidden, norm_gain, w_query, w_key, w_value, w_out, kv_cache, lengths, slot_owner, slot_page
):
    hbm = pl.BlockSpec(memory_space=pltpu.HBM)
    vmem = pl.BlockSpec(memory_space=pltpu.VMEM)
    mixed = pl.pallas_call(
        kernel,
        out_shape=jax.ShapeDtypeStruct((2, 64, HD), F32),
        in_specs=[hbm] * 10,
        out_specs=vmem,
        scratch_shapes=[
            pltpu.VMEM((64, 256), BF16),
            pltpu.VMEM((2, 64, HD), F32),
            pltpu.VMEM((256,), BF16),
            pltpu.VMEM((256, 1024), BF16),
            pltpu.VMEM((256, 256), BF16),
            pltpu.VMEM((1024, 256), BF16),
            pltpu.VMEM((32, 256, HD), BF16),
            pltpu.VMEM((32, 256, HD), BF16),
            pltpu.SMEM((32,), jnp.int32),
            pltpu.SMEM((32,), jnp.int32),
            pltpu.SMEM((32,), jnp.int32),
            pltpu.VMEM((N_INST, 16, HD), BF16),
            pltpu.VMEM((31, 16, HD), BF16),
            pltpu.VMEM((4, 32, HD), BF16),
            pltpu.VMEM((31, 32, HD), BF16),
            pltpu.VMEM((1, HD), F32),
            pltpu.VMEM((31, 1, HD), F32),
            pltpu.VMEM((N_INST, 16, HD), BF16),
            pltpu.VMEM((32, HD), BF16),
            pltpu.VMEM((512, 512), BF16),
            pltpu.VMEM((512, 512), BF16),
            pltpu.VMEM((32, 1, 256), F32),
            pltpu.VMEM((32, 1, HD), jnp.int32),
            pltpu.VMEM((N_INST, 16, HD), BF16),
            pltpu.VMEM((31, 16, HD), BF16),
            pltpu.VMEM((8, 2, HD), F32),
            pltpu.VMEM((31, 2, HD), F32),
            pltpu.VMEM((N_INST, 16, HD), BF16),
            pltpu.VMEM((N_TP, 64, 256), BF16),
            pltpu.SemaphoreType.DMA((11,)),
            pltpu.SemaphoreType.DMA((9,)),
            pltpu.SemaphoreType.DMA((9,)),
        ],
        compiler_params=pltpu.CompilerParams(
            collective_id=0, has_side_effects=True, vmem_limit_bytes=60 * 1024 * 1024
        ),
        name="paged_attention",
    )(
        hidden, norm_gain, w_query, w_key, w_value, w_out, kv_cache,
        lengths, slot_owner, slot_page,
    )
    return mixed.transpose(1, 0, 2).reshape(64, 256).astype(BF16)


def solution(mesh):
    return jax.shard_map(
        on_device,
        mesh=mesh,
        in_specs=(
            P(None, "inst"),
            P("inst"),
            P("inst", "tp"),
            P("inst", "tp"),
            P("inst", "tp"),
            P("tp", "inst"),
            P(None, "inst", None, "tp"),
            P(),
            P("inst"),
            P("inst"),
        ),
        out_specs=P(None, "inst"),
        check_vma=False,
    )
```

```python
import functools

import jax
import jax.numpy as jnp
from jax import lax
from jax.experimental import pallas as pl
from jax.experimental.pallas import tpu as pltpu
from jax.sharding import PartitionSpec as P

D = 8192
HD = 128
NEG = -1e30
EPS = 1e-05
THETA = 500000.0
SCALE = HD ** -0.5
N_INST = 32
N_TP = 8
MESH = pl.DeviceIdType.MESH
F32 = jnp.float32
BF16 = jnp.bfloat16


def iota(shape, dim):
    return lax.broadcasted_iota(jnp.int32, shape, dim)


def far_first():
    offsets = [(dz, dx) for dz in range(8) for dx in range(4) if dz or dx]
    return sorted(offsets, key=lambda o: -min(o[0], 8 - o[0]) - min(o[1], 4 - o[1]))


def rope(rows, cosine, sine):
    return rows * cosine + pltpu.roll(rows, 64, 1) * sine


def kernel(
    hid_hbm, gain_hbm, wq_hbm, wk_hbm, wv_hbm, wo_hbm, kv_hbm, len_hbm, own_hbm, page_hbm,
    out_ref,
    hid, hid32, gain, wq, wkv, wo, keys, vals, lens, owns, pages,
    q_src, q_rcv, kv_src, kv_rcv, sq_src, sq_rcv, q_all, kv_new,
    sel, sel_t, bias, member, acc_src, acc_rcv, st_src, st_rcv, att_all, tp_all,
    local_sem, send_sem, recv_sem,
):
    inst = lax.axis_index("inst")
    tp = lax.axis_index("tp")
    z, x = inst // 4, lax.rem(inst, 4)
    peers = [
        lax.rem(z + dz, 8) * 4 + lax.rem(x + dx, 4) for dz, dx in far_first()
    ]
    tp_peers = [lax.rem(tp + k, N_TP) for k in (4, 5, 3, 2, 6, 1, 7)]

    def local(i, src, dst):
        return pltpu.make_async_copy(src, dst, local_sem.at[i])

    loads = [
        local(0, hid_hbm, hid),
        local(1, wq_hbm, wq),
        local(2, wk_hbm, wkv.at[:, :HD]),
        local(3, wv_hbm, wkv.at[:, HD:]),
        local(4, own_hbm, owns),
        local(5, page_hbm, pages),
        local(6, len_hbm, lens),
        local(7, kv_hbm.at[0], keys),
        local(8, kv_hbm.at[1], vals),
        local(9, wo_hbm, wo),
        local(10, gain_hbm, gain),
    ]
    barrier = pltpu.get_barrier_semaphore()
    for to in peers:
        pl.semaphore_signal(barrier, inc=1, device_id={"inst": to}, device_id_type=MESH)
    for to in tp_peers:
        pl.semaphore_signal(barrier, inc=1, device_id={"tp": to}, device_id_type=MESH)
    for load in [loads[0], loads[10]] + loads[1:10]:
        load.start()

    def remote(src, dst, i, to, into=None):
        into = i if into is None else into
        return pltpu.make_async_remote_copy(
            src_ref=src, dst_ref=dst, send_sem=send_sem.at[i], recv_sem=recv_sem.at[into],
            device_id=to, device_id_type=MESH,
        )

    def arrived(ref, i):
        pltpu.make_async_copy(ref, ref, recv_sem.at[i]).wait()

    def departed(ref, i):
        pltpu.make_async_copy(ref, ref, send_sem.at[i]).wait()

    def drain(stage):
        if stage > 0:
            departed(sq_rcv, 0)
            departed(q_rcv, 1)

            @pl.when(z == 0)
            def _():
                departed(kv_src.at[0:3], 2)

            @pl.when(z > 0)
            def _():
                departed(kv_src, 2)

        if stage > 1:
            departed(q_rcv, 3)

            @pl.when(z == 0)
            def _():
                departed(kv_rcv.at[0:7], 4)

        if stage > 2:
            departed(st_rcv, 5)
            departed(acc_rcv, 6)
        if stage > 3:
            departed(acc_rcv, 7)
            departed(tp_all.at[0:7], 8)

    def place(to):
        return lax.rem(inst - to + (N_INST - 1), N_INST)

    places = [place(to) for to in peers]

    loads[0].wait()
    for c in range(2):
        hid32[c] = hid[:, HD * c : HD * c + HD].astype(F32)
    rows = jnp.concatenate(
        [
            jnp.concatenate(
                [hid32[c, pl.ds(16 * g + t, 8, stride=2), :] for g in range(4) for t in range(2)], axis=0
            )
            for c in range(2)
        ],
        axis=1,
    )
    squares = jnp.sum(rows * rows, axis=1, keepdims=True)
    spread = jnp.where(iota((64, HD), 0) == iota((64, HD), 1), squares, 0.0)
    sq_src[...] = jnp.sum(spread, axis=0, keepdims=True)
    loads[10].wait()
    normed = (rows * gain[...].astype(F32).reshape(1, 256)).astype(BF16)
    loads[1].wait()
    raw = jnp.dot(normed, wq[...], preferred_element_type=F32).astype(BF16)
    for h in range(8):
        for g in range(4):
            q_src[4 * h + g] = raw[16 * g : 16 * g + 16, HD * h : HD * h + HD]
    loads[2].wait()
    loads[3].wait()
    raw = jnp.dot(normed, wkv[...], preferred_element_type=F32).astype(BF16)
    for g in range(4):
        for k in range(2):
            kv_src[g, 16 * k : 16 * k + 16, :] = raw[16 * g : 16 * g + 16, HD * k : HD * k + HD]

    pl.semaphore_wait(barrier, N_INST - 1 + N_TP - 1)

    for to, there in zip(peers, places):
        remote(q_src.at[to], q_rcv.at[there], 1, {"inst": to}).start()
        remote(sq_src, sq_rcv.at[there], 0, {"inst": to}).start()
    for g in range(4):

        @pl.when(inst != g)
        def _():
            remote(kv_src.at[g], kv_rcv.at[place(g)], 2, {"inst": g}).start()

    loads[6].wait()
    spot = iota((16, HD), 0)
    lane = iota((16, HD), 1)
    position = jnp.zeros((16, HD), jnp.int32)
    for k in range(8):
        position = jnp.where(lax.rem(spot, 8) == k, lens[8 * x + k], position)
    position = position + spot // 8
    index = lax.rem(lane, 64).astype(F32)
    angle = position.astype(F32) * jnp.exp(index * (-2.0 / HD * 13.122363377404328))
    cosine = jnp.cos(angle)
    sine = jnp.sin(angle) * jnp.where(lane < 64, -1.0, 1.0)

    arrived(sq_rcv, 0)
    total = jnp.sum(sq_rcv[...], axis=0) + sq_src[...]
    mine = jnp.where(lane == 16 * x + spot, total, 0.0)
    inverse = lax.rsqrt(jnp.sum(mine, axis=1, keepdims=True) / D + EPS)
    arrived(q_rcv, 1)
    joined = jnp.sum(q_rcv[...].astype(F32), axis=0) + q_src[inst].astype(F32)
    q_all[inst] = rope(joined * inverse, cosine, sine).astype(BF16)
    for to in peers:
        remote(q_all.at[inst], q_all.at[inst], 3, {"inst": to}).start()

    loads[4].wait()
    loads[5].wait()
    row = iota((16, 512), 0)
    shifted = iota((16, 512), 1) - ((row // 2) * 64 + lax.rem(row, 2) * 8)
    column = iota((1, 512), 1)

    def slot(s, targets):
        owner = owns[s]
        safe = jnp.maximum(owner, 0)
        target = jnp.where(owner >= 0, (safe // 8) * 16 + lax.rem(safe, 8), -1000)
        limit = jnp.where(owner >= 0, lens[safe] - pages[s] * 256, 0)
        sel[pl.ds(pl.multiple_of(16 * s, 16), 16), :] = (shifted == target).astype(F32).astype(BF16)
        bias[s] = jnp.where(iota((1, 256), 1) < limit, 0.0, NEG)
        member[s] = (iota((1, HD), 1) == owner).astype(jnp.int32)
        return jnp.where(column // 16 == s, target, targets)

    targets = lax.fori_loop(0, 32, slot, jnp.zeros((1, 512), jnp.int32), unroll=4)
    j = lax.rem(column, 16)
    targets = targets + (j // 2) * 64 + lax.rem(j, 2) * 8
    turned = lax.rem(iota((512, 512), 0) + 64 * lax.rem(z + 2, 8), 512)
    sel_t[...] = (turned == targets).astype(F32).astype(BF16)

    @pl.when(z == 0)
    def _():
        arrived(kv_rcv, 2)
        both = jnp.sum(kv_rcv[...].astype(F32), axis=0) + kv_src[inst].astype(F32)
        both = both * jnp.concatenate([inverse, inverse], axis=0)
        kv_new[0:16, :] = rope(both[0:16], cosine, sine).astype(BF16)
        kv_new[16:32, :] = both[16:32].astype(BF16)
        for k in range(1, 8):
            remote(kv_new, kv_new, 4, {"inst": 4 * k + x}).start()

    loads[7].wait()
    loads[8].wait()
    arrived(q_all.at[0:31], 3)
    queries = jnp.dot(sel[...], q_all[...].reshape(512, HD), preferred_element_type=F32).astype(BF16)
    scores = lax.dot_general(
        queries.reshape(32, 16, HD), keys[...], (((2,), (2,)), ((0,), (0,))), preferred_element_type=F32
    )
    scores = scores * SCALE + bias[...]
    top = jnp.max(scores, axis=2, keepdims=True)
    weights = jnp.exp(scores - top)
    weight_sum = jnp.sum(weights, axis=2, keepdims=True)
    part = lax.dot_general(
        weights.astype(BF16), vals[...], (((2,), (1,)), ((0,), (0,))), preferred_element_type=F32
    )
    belongs = member[...] > 0
    top_req = jnp.max(jnp.where(belongs, top, NEG), axis=0)
    peak = jnp.max(jnp.where(belongs, top_req[None], NEG), axis=2, keepdims=True)
    factor = jnp.exp(top - peak)
    sum_req = jnp.sum(jnp.where(belongs, factor * weight_sum, 0.0), axis=0)
    stats = jnp.where(iota((16, HD), 1) < 32, top_req, pltpu.roll(sum_req, 32, 1))
    st_src[...] = stats.reshape(8, 2, HD)
    part = (part * factor).reshape(512, HD)
    high = part.astype(BF16)
    low = (part - high.astype(F32)).astype(BF16)
    parts = jnp.concatenate([high, low], axis=1)

    def send_stats(dz, dx):
        to = lax.rem(z + dz, 8) * 4 + lax.rem(x + dx, 4)
        remote(st_src.at[lax.rem(z + dz, 8)], st_rcv.at[place(to)], 5, {"inst": to}).start()

    def send_part(dz, dx):
        to = lax.rem(z + dz, 8) * 4 + lax.rem(x + dx, 4)
        held = acc_src.at[4 * ((dz - 2) % 8) + lax.rem(x + dx, 4)]
        remote(held, acc_rcv.at[place(to)], 6, {"inst": to}).start()

    for half in range(2):
        rows = slice(256 * half, 256 * half + 256)
        both = jnp.dot(sel_t[rows, :], parts, preferred_element_type=F32)
        both = (both[:, :HD] + both[:, HD:]).astype(BF16)
        acc_src[16 * half : 16 * half + 16] = both.reshape(16, 16, HD)
        for dz, dx in far_first():
            if ((dz - 2) % 8 >= 4) == half:
                send_part(dz, dx)
                send_stats(dz, dx)

    @pl.when(z > 0)
    def _():
        arrived(kv_new, 4)

    row = iota((16, 16), 0)
    key = iota((16, 16), 1)
    seen = (lax.rem(row, 8) == lax.rem(key, 8)) & (key // 8 <= row // 8)
    fresh = lax.dot_general(
        q_all[inst], kv_new[0:16, :], (((1,), (1,)), ((), ())), preferred_element_type=F32
    ) * SCALE
    fresh = jnp.where(seen, fresh, NEG)
    fresh_top = jnp.max(fresh, axis=1, keepdims=True)
    weights = jnp.where(seen, jnp.exp(fresh - fresh_top), 0.0)
    fresh_sum = jnp.sum(weights, axis=1, keepdims=True)
    fresh_out = jnp.dot(weights.astype(BF16), kv_new[16:32, :], preferred_element_type=F32)

    arrived(st_rcv, 5)
    own = st_src[pl.ds(z, 1)]
    stats = jnp.concatenate(
        [st_rcv[:, 0, :], own[:, 0, :], st_rcv[:, 1, :], own[:, 1, :]], axis=0
    )
    stats = pltpu.roll(stats, lax.rem(HD - 8 * x, HD), 1).T
    tops, sums = stats[0:8], stats[32:40]
    scales, fresh_scales, totals = [], [], []
    for t in range(2):
        first = fresh_top[8 * t : 8 * t + 8]
        held = tops[:, 32 * t : 32 * t + 32]
        peak = jnp.maximum(jnp.max(held, axis=1, keepdims=True), first)
        scale = jnp.exp(held - peak)
        fresh_scale = jnp.exp(first - peak)
        total = jnp.sum(scale * sums[:, 32 * t : 32 * t + 32], axis=1, keepdims=True)
        totals.append(total + fresh_scale * fresh_sum[8 * t : 8 * t + 8])
        scales.append(scale)
        fresh_scales.append(fresh_scale)
    scale = jnp.concatenate(scales, axis=0)
    arrived(acc_rcv, 6)
    out = jnp.concatenate(fresh_scales, axis=0) * fresh_out
    for d in range(N_INST):
        held = acc_rcv[d] if d < N_INST - 1 else acc_src[24 + x]
        out = out + scale[:, d : d + 1] * held.astype(F32)
    att_all[x, z] = (out / jnp.concatenate(totals, axis=0)).astype(BF16)
    for k in range(N_INST - 1):
        to = k + (k >= inst).astype(jnp.int32)
        group = lax.rem(x - lax.rem(to, 4) + 4, 4)
        remote(att_all.at[x, z], att_all.at[x, z], 7, {"inst": to}, 7 + group).start()

    loads[9].wait()
    for k in (0, 1, 3, 2):
        g = lax.rem(x + k, 4)
        arrived(att_all.at[g] if k else att_all.at[g, 0:7], 7 + k)
        attention = jnp.concatenate([att_all[g, h] for h in range(8)], axis=1)
        tp_all[tp, g] = jnp.dot(attention, wo[...], preferred_element_type=F32).astype(BF16)
        for to in tp_peers:
            remote(tp_all.at[tp, g], tp_all.at[tp, g], 8, {"tp": to}, 11 + k).start()
    for k in (0, 1, 3, 2):
        g = lax.rem(x + k, 4)
        arrived(tp_all.at[0:7, g], 11 + k)
        mixed = tp_all[0, g].astype(F32)
        for d in range(1, N_TP):
            mixed = mixed + tp_all[d, g].astype(F32)
        for t in range(2):
            for c in range(2):
                held = mixed[8 * t : 8 * t + 8, HD * c : HD * c + HD]
                out_ref[c, g, pl.ds(t, 8, stride=2), :] = held

    drain(4)


def on_device(*arrays):
    hbm = pl.BlockSpec(memory_space=pltpu.HBM)
    vmem = pl.BlockSpec(memory_space=pltpu.VMEM)
    mixed = pl.pallas_call(
        kernel,
        out_shape=pltpu.VMEM((2, 4, 16, HD), F32),
        in_specs=[hbm] * 10,
        out_specs=vmem,
        scratch_shapes=[
            pltpu.VMEM((64, 256), BF16),
            pltpu.VMEM((2, 64, HD), F32),
            pltpu.VMEM((256,), BF16),
            pltpu.VMEM((256, 1024), BF16),
            pltpu.VMEM((256, 256), BF16),
            pltpu.VMEM((1024, 256), BF16),
            pltpu.VMEM((32, 256, HD), BF16),
            pltpu.VMEM((32, 256, HD), BF16),
            pltpu.SMEM((32,), jnp.int32),
            pltpu.SMEM((32,), jnp.int32),
            pltpu.SMEM((32,), jnp.int32),
            pltpu.VMEM((N_INST, 16, HD), BF16),
            pltpu.VMEM((31, 16, HD), BF16),
            pltpu.VMEM((4, 32, HD), BF16),
            pltpu.VMEM((31, 32, HD), BF16),
            pltpu.VMEM((1, HD), F32),
            pltpu.VMEM((31, 1, HD), F32),
            pltpu.VMEM((N_INST, 16, HD), BF16),
            pltpu.VMEM((32, HD), BF16),
            pltpu.VMEM((512, 512), BF16),
            pltpu.VMEM((512, 512), BF16),
            pltpu.VMEM((32, 1, 256), F32),
            pltpu.VMEM((32, 1, HD), jnp.int32),
            pltpu.VMEM((N_INST, 16, HD), BF16),
            pltpu.VMEM((31, 16, HD), BF16),
            pltpu.VMEM((8, 2, HD), F32),
            pltpu.VMEM((31, 2, HD), F32),
            pltpu.VMEM((4, 8, 16, HD), BF16),
            pltpu.VMEM((N_TP, 4, 16, 256), BF16),
            pltpu.SemaphoreType.DMA((11,)),
            pltpu.SemaphoreType.DMA((9,)),
            pltpu.SemaphoreType.DMA((15,)),
        ],
        compiler_params=pltpu.CompilerParams(
            collective_id=0, has_side_effects=True, vmem_limit_bytes=48 * 1024 * 1024
        ),
        name="paged_attention",
    )(*(pltpu.with_memory_space_constraint(a, pltpu.HBM) for a in arrays))
    return mixed.transpose(1, 2, 0, 3).reshape(64, 256).astype(BF16)


def solution(mesh):
    return jax.shard_map(
        on_device,
        mesh=mesh,
        in_specs=(
            P(None, "inst"),
            P("inst"),
            P("inst", "tp"),
            P("inst", "tp"),
            P("inst", "tp"),
            P("tp", "inst"),
            P(None, "inst", None, "tp"),
            P(),
            P("inst"),
            P("inst"),
        ),
        out_specs=P(None, "inst"),
        check_vma=False,
    )
```

```python
import functools

import jax
import jax.numpy as jnp
from jax import lax
from jax.experimental import pallas as pl
from jax.experimental.pallas import tpu as pltpu
from jax.sharding import PartitionSpec as P

D = 8192
HD = 128
NEG = -1e30
EPS = 1e-05
THETA = 500000.0
SCALE = HD ** -0.5
N_INST = 32
N_TP = 8
MESH = pl.DeviceIdType.MESH
F32 = jnp.float32
BF16 = jnp.bfloat16


def iota(shape, dim):
    return lax.broadcasted_iota(jnp.int32, shape, dim)


def far_first():
    offsets = [(dz, dx) for dz in range(8) for dx in range(4) if dz or dx]
    return sorted(offsets, key=lambda o: -min(o[0], 8 - o[0]) - min(o[1], 4 - o[1]))


def rope(rows, cosine, sine):
    return rows * cosine + pltpu.roll(rows, 64, 1) * sine


def kernel(
    hid_hbm, gain_hbm, wq_hbm, wk_hbm, wv_hbm, wo_hbm, kv_hbm, len_hbm, own_hbm, page_hbm,
    out_ref,
    hid, hid32, gain, wq, wkv, wo, keys, vals, lens, owns, pages,
    q_src, q_rcv, kv_src, kv_rcv, sq_src, sq_rcv, q_all, q_low, kv_new,
    sel, sel_t, bias, member, acc_src, acc_rcv, st_src, st_rcv, att_all, tp_all,
    local_sem, send_sem, recv_sem,
):
    inst = lax.axis_index("inst")
    tp = lax.axis_index("tp")
    z, x = inst // 4, lax.rem(inst, 4)
    core, y = lax.rem(tp, 2), tp // 2
    low = tp - core
    high = low + 1
    is_low, is_high = core == 0, core == 1
    offsets = far_first()
    peers = [lax.rem(z + dz, 8) * 4 + lax.rem(x + dx, 4) for dz, dx in offsets]
    tp_peers = [lax.rem(tp + k, N_TP) for k in (4, 5, 3, 2, 6, 1, 7)]

    def local(i, src, dst):
        return pltpu.make_async_copy(src, dst, local_sem.at[i])

    loads = [
        local(0, hid_hbm, hid),
        local(1, wq_hbm, wq),
        local(2, wk_hbm, wkv.at[:, :HD]),
        local(3, wv_hbm, wkv.at[:, HD:]),
        local(4, own_hbm, owns),
        local(5, page_hbm, pages),
        local(6, len_hbm, lens),
        local(7, kv_hbm.at[0], keys),
        local(8, kv_hbm.at[1], vals),
        local(9, wo_hbm, wo.at[1]),
        local(10, gain_hbm, gain),
    ]
    barrier = pltpu.get_barrier_semaphore()

    def greet(to):
        pl.semaphore_signal(barrier, inc=1, device_id=to, device_id_type=MESH)

    @pl.when(is_high)
    def _():
        for to in peers:
            greet({"inst": to, "tp": tp})
            greet({"inst": to, "tp": low})

    for to in tp_peers:
        greet({"inst": inst, "tp": to})
    for load in [loads[0], loads[10]] + loads[1:9]:
        load.start()

    def remote(src, dst, i, to, into):
        return pltpu.make_async_remote_copy(
            src_ref=src, dst_ref=dst, send_sem=send_sem.at[i], recv_sem=recv_sem.at[into],
            device_id=to, device_id_type=MESH,
        )

    def arrived(ref, i):
        pltpu.make_async_copy(ref, ref, recv_sem.at[i]).wait()

    def departed(ref, i):
        pltpu.make_async_copy(ref, ref, send_sem.at[i]).wait()

    loads[0].wait()
    for c in range(2):
        hid32[c] = hid[:, HD * c : HD * c + HD].astype(F32)
    rows = jnp.concatenate(
        [
            jnp.concatenate(
                [hid32[c, pl.ds(16 * g + t, 8, stride=2), :] for g in range(4) for t in range(2)], axis=0
            )
            for c in range(2)
        ],
        axis=1,
    )
    squares = jnp.sum(rows * rows, axis=1, keepdims=True)
    spread = jnp.where(iota((64, HD), 0) == iota((64, HD), 1), squares, 0.0)
    sq_src[...] = jnp.sum(spread, axis=0, keepdims=True)
    loads[10].wait()
    normed = (rows * gain[...].astype(F32).reshape(1, 256)).astype(BF16)
    loads[1].wait()
    raw = jnp.dot(normed, wq[...], preferred_element_type=F32).astype(BF16)
    for h in range(8):
        for g in range(4):
            q_src[4 * h + g] = raw[16 * g : 16 * g + 16, HD * h : HD * h + HD]
    loads[2].wait()
    loads[3].wait()
    raw = jnp.dot(normed, wkv[...], preferred_element_type=F32).astype(BF16)
    for g in range(4):
        for k in range(2):
            kv_src[g, 16 * k : 16 * k + 16, :] = raw[16 * g : 16 * g + 16, HD * k : HD * k + HD]

    pl.semaphore_wait(barrier, N_INST - 1 + N_TP - 1)

    @pl.when(is_low)
    def _():
        for to in peers:
            remote(q_src.at[to], q_rcv.at[0, inst], 1, {"inst": to, "tp": high}, 0).start()
        remote(q_src.at[inst], q_rcv.at[0, inst], 1, {"inst": inst, "tp": high}, 0).start()

    @pl.when(is_high)
    def _():
        for to in peers:
            remote(q_src.at[to], q_rcv.at[1, inst], 1, {"inst": to, "tp": tp}, 1).start()
            remote(sq_src, sq_rcv.at[inst], 0, {"inst": to, "tp": tp}, 5).start()
        q_rcv[1, inst] = q_src[inst]
        sq_rcv[inst] = sq_src[...]

    for g in range(4):

        @pl.when((inst != g) | is_low)
        def _():
            remote(kv_src.at[g], kv_rcv.at[core, inst], 2, {"inst": g, "tp": high}, 2 + core).start()

    @pl.when(is_low)
    def _():
        remote(wo_hbm, wo.at[0], 9, {"inst": inst, "tp": high}, 7).start()

    loads[6].wait()

    loads[4].wait()
    loads[5].wait()
    row = iota((16, 512), 0)
    shifted = iota((16, 512), 1) - ((row // 2) * 64 + lax.rem(row, 2) * 8)
    column = iota((1, 512), 1)

    def slot(s, targets):
        owner = owns[s]
        safe = jnp.maximum(owner, 0)
        target = jnp.where(owner >= 0, (safe // 8) * 16 + lax.rem(safe, 8), -1000)
        limit = jnp.where(owner >= 0, lens[safe] - pages[s] * 256, 0)
        sel[pl.ds(pl.multiple_of(16 * s, 16), 16), :] = (shifted == target).astype(F32).astype(BF16)
        bias[s] = jnp.where(iota((1, 256), 1) < limit, 0.0, NEG)
        member[s] = (iota((1, HD), 1) == owner).astype(jnp.int32)
        return jnp.where(column // 16 == s, target, targets)

    targets = lax.fori_loop(0, 32, slot, jnp.zeros((1, 512), jnp.int32), unroll=4)
    j = lax.rem(column, 16)
    targets = targets + (j // 2) * 64 + lax.rem(j, 2) * 8
    turned = lax.rem(iota((512, 512), 0) + 64 * lax.rem(z + 2, 8), 512)
    sel_t[...] = (turned == targets).astype(F32).astype(BF16)

    @pl.when(is_high)
    def _():
        loads[9].start()
        spot = iota((16, HD), 0)
        lane = iota((16, HD), 1)
        position = jnp.zeros((16, HD), jnp.int32)
        for k in range(8):
            position = jnp.where(lax.rem(spot, 8) == k, lens[8 * x + k], position)
        position = position + spot // 8
        index = lax.rem(lane, 64).astype(F32)
        angle = position.astype(F32) * jnp.exp(index * (-2.0 / HD * 13.122363377404328))
        cosine = jnp.cos(angle)
        sine = jnp.sin(angle) * jnp.where(lane < 64, -1.0, 1.0)
        arrived(sq_rcv.at[0:31], 5)
        total = jnp.sum(sq_rcv[...], axis=0)
        mine = jnp.where(lane == 16 * x + spot, total, 0.0)
        inverse = lax.rsqrt(jnp.sum(mine, axis=1, keepdims=True) / D + EPS)
        arrived(q_rcv.at[1, 0:31], 1)
        joined = jnp.sum(q_rcv[1].astype(F32), axis=0)
        q_all[inst] = rope(joined * inverse, cosine, sine).astype(BF16)
        for to in peers:
            remote(q_all.at[inst], q_all.at[inst], 10, {"inst": to, "tp": tp}, 4).start()
        arrived(q_rcv.at[0], 0)
        joined = jnp.sum(q_rcv[0].astype(F32), axis=0)
        q_low[...] = rope(joined * inverse, cosine, sine).astype(BF16)
        for to in peers:
            remote(q_low, q_all.at[inst], 3, {"inst": to, "tp": low}, 4).start()
        remote(q_low, q_all.at[inst], 3, {"inst": inst, "tp": low}, 4).start()

        @pl.when(z == 0)
        def _():
            kv_rcv[1, inst] = kv_src[x]
            arrived(kv_rcv.at[0], 2)
            arrived(kv_rcv.at[1, 0:31], 3)
            for c in range(2):
                both = jnp.sum(kv_rcv[c].astype(F32), axis=0)
                both = both * jnp.concatenate([inverse, inverse], axis=0)
                kv_new[c, 0:16, :] = rope(both[0:16], cosine, sine).astype(BF16)
                kv_new[c, 16:32, :] = both[16:32].astype(BF16)
            for k in range(1, 8):
                remote(kv_new, kv_new, 4, {"inst": 4 * k + x, "tp": tp}, 6).start()

    loads[7].wait()
    loads[8].wait()

    @pl.when(is_low)
    def _():
        arrived(q_all, 4)

    @pl.when(is_high)
    def _():
        arrived(q_all.at[0:31], 4)

    queries = jnp.dot(sel[...], q_all[...].reshape(512, HD), preferred_element_type=F32).astype(BF16)
    scores = lax.dot_general(
        queries.reshape(32, 16, HD), keys[...], (((2,), (2,)), ((0,), (0,))), preferred_element_type=F32
    )
    scores = scores * SCALE + bias[...]
    top = jnp.max(scores, axis=2, keepdims=True)
    weights = jnp.exp(scores - top)
    weight_sum = jnp.sum(weights, axis=2, keepdims=True)
    part = lax.dot_general(
        weights.astype(BF16), vals[...], (((2,), (1,)), ((0,), (0,))), preferred_element_type=F32
    )
    belongs = member[...] > 0
    top_req = jnp.max(jnp.where(belongs, top, NEG), axis=0)
    peak = jnp.max(jnp.where(belongs, top_req[None], NEG), axis=2, keepdims=True)
    factor = jnp.exp(top - peak)
    sum_req = jnp.sum(jnp.where(belongs, factor * weight_sum, 0.0), axis=0)
    stats = jnp.where(iota((16, HD), 1) < 32, top_req, pltpu.roll(sum_req, 32, 1))
    st_src[...] = stats.reshape(8, 2, HD)
    part = (part * factor).reshape(512, HD)
    high_part = part.astype(BF16)
    low_part = (part - high_part.astype(F32)).astype(BF16)
    parts = jnp.concatenate([high_part, low_part], axis=1)

    def send_part(dz, dx):
        zo, xo = lax.rem(z + dz, 8), lax.rem(x + dx, 4)
        to = {"inst": zo * 4 + xo, "tp": high}
        held = acc_src.at[4 * ((dz - 2) % 8) + xo]
        remote(held, acc_rcv.at[core, inst], 6, to, 10 + core).start()
        remote(st_src.at[zo], st_rcv.at[core, inst], 5, to, 8 + core).start()

    for half in range(2):
        rows = slice(256 * half, 256 * half + 256)
        both = jnp.dot(sel_t[rows, :], parts, preferred_element_type=F32)
        both = (both[:, :HD] + both[:, HD:]).astype(BF16)
        acc_src[16 * half : 16 * half + 16] = both.reshape(16, 16, HD)
        for dz, dx in offsets:
            if ((dz - 2) % 8 >= 4) == half:
                send_part(dz, dx)

    @pl.when(is_low)
    def _():
        send_part(0, 0)

    @pl.when(is_high)
    def _():
        acc_rcv[1, inst] = acc_src[24 + x]
        st_rcv[1, inst] = st_src[z]

        @pl.when(z > 0)
        def _():
            arrived(kv_new, 6)

        row = iota((16, 16), 0)
        key = iota((16, 16), 1)
        seen = (lax.rem(row, 8) == lax.rem(key, 8)) & (key // 8 <= row // 8)
        fresh_tops, fresh_sums, fresh_outs = [], [], []
        for c in range(2):
            query = q_all[inst] if c else q_low[...]
            fresh = lax.dot_general(
                query, kv_new[c, 0:16, :], (((1,), (1,)), ((), ())), preferred_element_type=F32
            ) * SCALE
            fresh = jnp.where(seen, fresh, NEG)
            fresh_top = jnp.max(fresh, axis=1, keepdims=True)
            weights = jnp.where(seen, jnp.exp(fresh - fresh_top), 0.0)
            fresh_tops.append(fresh_top)
            fresh_sums.append(jnp.sum(weights, axis=1, keepdims=True))
            fresh_outs.append(
                jnp.dot(weights.astype(BF16), kv_new[c, 16:32, :], preferred_element_type=F32)
            )

        for c in (1, 0):
            arrived(st_rcv.at[1, 0:31] if c else st_rcv.at[0], 8 + c)
            stats = jnp.concatenate([st_rcv[c, :, 0, :], st_rcv[c, :, 1, :]], axis=0)
            stats = pltpu.roll(stats, lax.rem(HD - 8 * x, HD), 1).T
            tops, sums = stats[0:8], stats[32:40]
            scales, fresh_scales, totals = [], [], []
            for t in range(2):
                first = fresh_tops[c][8 * t : 8 * t + 8]
                held = tops[:, 32 * t : 32 * t + 32]
                peak = jnp.maximum(jnp.max(held, axis=1, keepdims=True), first)
                scale = jnp.exp(held - peak)
                fresh_scale = jnp.exp(first - peak)
                total = jnp.sum(scale * sums[:, 32 * t : 32 * t + 32], axis=1, keepdims=True)
                totals.append(total + fresh_scale * fresh_sums[c][8 * t : 8 * t + 8])
                scales.append(scale)
                fresh_scales.append(fresh_scale)
            scale = jnp.concatenate(scales, axis=0)
            arrived(acc_rcv.at[1, 0:31] if c else acc_rcv.at[0], 10 + c)
            out = jnp.concatenate(fresh_scales, axis=0) * fresh_outs[c]
            for d in range(N_INST):
                out = out + scale[:, d : d + 1] * acc_rcv[c, d].astype(F32)
            att_all[x, z, c] = (out / jnp.concatenate(totals, axis=0)).astype(BF16)

        for k in range(N_INST - 1):
            to = k + (k >= inst).astype(jnp.int32)
            group = lax.rem(x - lax.rem(to, 4) + 4, 4)
            remote(att_all.at[x, z], att_all.at[x, z], 7, {"inst": to, "tp": tp}, 12 + group).start()

        loads[9].wait()
        arrived(wo.at[0], 7)
        for k in (0, 1, 3, 2):
            g = lax.rem(x + k, 4)
            arrived(att_all.at[g] if k else att_all.at[g, 0:7], 12 + k)
            attention = jnp.concatenate([att_all[g, h, c] for c in range(2) for h in range(8)], axis=1)
            projected = jnp.dot(attention, wo[...].reshape(2048, 256), preferred_element_type=F32)
            tp_all[y, g] = projected.astype(BF16)
            for to in tp_peers:
                remote(tp_all.at[y, g], tp_all.at[y, g], 8, {"inst": inst, "tp": to}, 16 + k).start()

    for k in (0, 1, 3, 2):
        g = lax.rem(x + k, 4)

        @pl.when(is_low)
        def _():
            arrived(tp_all.at[:, g], 16 + k)

        @pl.when(is_high)
        def _():
            arrived(tp_all.at[0:3, g], 16 + k)

        mixed = tp_all[0, g].astype(F32)
        for d in range(1, 4):
            mixed = mixed + tp_all[d, g].astype(F32)
        for t in range(2):
            for c in range(2):
                held = mixed[8 * t : 8 * t + 8, HD * c : HD * c + HD]
                out_ref[c, g, pl.ds(t, 8, stride=2), :] = held

    @pl.when(is_low)
    def _():
        departed(q_rcv.at[0], 1)
        departed(kv_src, 2)
        departed(st_rcv.at[0], 5)
        departed(acc_rcv.at[0], 6)
        departed(wo.at[0], 9)

    @pl.when(is_high)
    def _():
        departed(sq_rcv.at[0:31], 0)
        departed(q_rcv.at[1, 0:31], 1)

        @pl.when(z == 0)
        def _():
            departed(kv_src.at[0:3], 2)
            departed(kv_rcv.at[0, 0:14], 4)

        @pl.when(z > 0)
        def _():
            departed(kv_src, 2)

        departed(q_rcv.at[0], 3)
        departed(q_rcv.at[1, 0:31], 10)
        departed(st_rcv.at[1, 0:31], 5)
        departed(acc_rcv.at[1, 0:31], 6)
        departed(acc_rcv.at[:, 0:31], 7)
        departed(wo.at[0, 0:448], 8)


def on_device(*arrays):
    hbm = pl.BlockSpec(memory_space=pltpu.HBM)
    vmem = pl.BlockSpec(memory_space=pltpu.VMEM)
    mixed = pl.pallas_call(
        kernel,
        out_shape=pltpu.VMEM((2, 4, 16, HD), F32),
        in_specs=[hbm] * 10,
        out_specs=vmem,
        scratch_shapes=[
            pltpu.VMEM((64, 256), BF16),
            pltpu.VMEM((2, 64, HD), F32),
            pltpu.VMEM((256,), BF16),
            pltpu.VMEM((256, 1024), BF16),
            pltpu.VMEM((256, 256), BF16),
            pltpu.VMEM((2, 1024, 256), BF16),
            pltpu.VMEM((32, 256, HD), BF16),
            pltpu.VMEM((32, 256, HD), BF16),
            pltpu.SMEM((32,), jnp.int32),
            pltpu.SMEM((32,), jnp.int32),
            pltpu.SMEM((32,), jnp.int32),
            pltpu.VMEM((N_INST, 16, HD), BF16),
            pltpu.VMEM((2, N_INST, 16, HD), BF16),
            pltpu.VMEM((4, 32, HD), BF16),
            pltpu.VMEM((2, N_INST, 32, HD), BF16),
            pltpu.VMEM((1, HD), F32),
            pltpu.VMEM((N_INST, 1, HD), F32),
            pltpu.VMEM((N_INST, 16, HD), BF16),
            pltpu.VMEM((16, HD), BF16),
            pltpu.VMEM((2, 32, HD), BF16),
            pltpu.VMEM((512, 512), BF16),
            pltpu.VMEM((512, 512), BF16),
            pltpu.VMEM((32, 1, 256), F32),
            pltpu.VMEM((32, 1, HD), jnp.int32),
            pltpu.VMEM((N_INST, 16, HD), BF16),
            pltpu.VMEM((2, N_INST, 16, HD), BF16),
            pltpu.VMEM((8, 2, HD), F32),
            pltpu.VMEM((2, N_INST, 2, HD), F32),
            pltpu.VMEM((4, 8, 2, 16, HD), BF16),
            pltpu.VMEM((4, 4, 16, 256), BF16),
            pltpu.SemaphoreType.DMA((11,)),
            pltpu.SemaphoreType.DMA((11,)),
            pltpu.SemaphoreType.DMA((20,)),
        ],
        compiler_params=pltpu.CompilerParams(
            collective_id=0, has_side_effects=True, vmem_limit_bytes=48 * 1024 * 1024
        ),
        name="paged_attention",
    )(*(pltpu.with_memory_space_constraint(a, pltpu.HBM) for a in arrays))
    return mixed.transpose(1, 2, 0, 3).reshape(64, 256).astype(BF16)


def solution(mesh):
    return jax.shard_map(
        on_device,
        mesh=mesh,
        in_specs=(
            P(None, "inst"),
            P("inst"),
            P("inst", "tp"),
            P("inst", "tp"),
            P("inst", "tp"),
            P("tp", "inst"),
            P(None, "inst", None, "tp"),
            P(),
            P("inst"),
            P("inst"),
        ),
        out_specs=P(None, "inst"),
        check_vma=False,
    )
```

```python
import functools

import jax
import jax.numpy as jnp
from jax import lax
from jax.experimental import pallas as pl
from jax.experimental.pallas import tpu as pltpu
from jax.sharding import PartitionSpec as P

D = 8192
HD = 128
NEG = -1e30
EPS = 1e-05
THETA = 500000.0
SCALE = HD ** -0.5
N_INST = 32
N_TP = 8
MESH = pl.DeviceIdType.MESH
F32 = jnp.float32
BF16 = jnp.bfloat16


def iota(shape, dim):
    return lax.broadcasted_iota(jnp.int32, shape, dim)


def far_first():
    offsets = [(dz, dx) for dz in range(8) for dx in range(4) if dz or dx]
    return sorted(offsets, key=lambda o: -min(o[0], 8 - o[0]) - min(o[1], 4 - o[1]))


def rope(rows, cosine, sine):
    return rows * cosine + pltpu.roll(rows, 64, 1) * sine


def kernel(
    hid_hbm, gain_hbm, wq_hbm, wk_hbm, wv_hbm, wo_hbm, kv_hbm, len_hbm, own_hbm, page_hbm,
    out_ref,
    hid, hid32, gain, wq, wkv, wo, keys, vals, lens, owns, pages,
    q_src, q_rcv, kv_src, kv_rcv, sq_src, sq_rcv, q_all, q_low, kv_new,
    sel, sel_t, bias, member, acc_src, acc_rcv, st_src, st_rcv, att_all, tp_all,
    local_sem, send_sem, recv_sem,
):
    inst = lax.axis_index("inst")
    tp = lax.axis_index("tp")
    z, x = inst // 4, lax.rem(inst, 4)
    core, y = lax.rem(tp, 2), tp // 2
    low = tp - core
    high = low + 1
    is_low, is_high = core == 0, core == 1
    offsets = far_first()
    peers = [lax.rem(z + dz, 8) * 4 + lax.rem(x + dx, 4) for dz, dx in offsets]
    tp_peers = [lax.rem(tp + k, N_TP) for k in (4, 5, 3, 2, 6, 1, 7)]

    def local(i, src, dst):
        return pltpu.make_async_copy(src, dst, local_sem.at[i])

    loads = [
        local(0, hid_hbm, hid),
        local(1, wq_hbm, wq),
        local(2, wk_hbm, wkv.at[:, :HD]),
        local(3, wv_hbm, wkv.at[:, HD:]),
        local(4, own_hbm, owns),
        local(5, page_hbm, pages),
        local(6, len_hbm, lens),
        local(7, kv_hbm.at[0], keys),
        local(8, kv_hbm.at[1], vals),
        local(9, wo_hbm, wo.at[1]),
        local(10, gain_hbm, gain),
    ]
    barrier = pltpu.get_barrier_semaphore()

    def greet(to):
        pl.semaphore_signal(barrier, inc=1, device_id=to, device_id_type=MESH)

    @pl.when(is_high)
    def _():
        for to in peers:
            greet({"inst": to, "tp": tp})
            greet({"inst": to, "tp": low})

    for to in tp_peers:
        greet({"inst": inst, "tp": to})
    for load in [loads[0], loads[10]] + loads[1:9]:
        load.start()

    def remote(src, dst, i, to, into):
        return pltpu.make_async_remote_copy(
            src_ref=src, dst_ref=dst, send_sem=send_sem.at[i], recv_sem=recv_sem.at[into],
            device_id=to, device_id_type=MESH,
        )

    def arrived(ref, i):
        pltpu.make_async_copy(ref, ref, recv_sem.at[i]).wait()

    def departed(ref, i):
        pltpu.make_async_copy(ref, ref, send_sem.at[i]).wait()

    loads[0].wait()
    for c in range(2):
        hid32[c] = hid[:, HD * c : HD * c + HD].astype(F32)
    rows = jnp.concatenate(
        [
            jnp.concatenate(
                [hid32[c, pl.ds(16 * g + t, 8, stride=2), :] for g in range(4) for t in range(2)], axis=0
            )
            for c in range(2)
        ],
        axis=1,
    )
    squares = jnp.sum(rows * rows, axis=1, keepdims=True)
    spread = jnp.where(iota((64, HD), 0) == iota((64, HD), 1), squares, 0.0)
    sq_src[...] = jnp.sum(spread, axis=0, keepdims=True)
    loads[10].wait()
    normed = (rows * gain[...].astype(F32).reshape(1, 256)).astype(BF16)
    loads[1].wait()
    raw = jnp.dot(normed, wq[...], preferred_element_type=F32).astype(BF16)
    for h in range(8):
        for g in range(4):
            q_src[4 * h + g] = raw[16 * g : 16 * g + 16, HD * h : HD * h + HD]
    loads[2].wait()
    loads[3].wait()
    raw = jnp.dot(normed, wkv[...], preferred_element_type=F32).astype(BF16)
    for g in range(4):
        for k in range(2):
            kv_src[g, 16 * k : 16 * k + 16, :] = raw[16 * g : 16 * g + 16, HD * k : HD * k + HD]

    pl.semaphore_wait(barrier, N_INST - 1 + N_TP - 1)

    @pl.when(is_low)
    def _():
        for to in peers:
            remote(q_src.at[to], q_rcv.at[0, inst], 1, {"inst": to, "tp": high}, 0).start()
        remote(q_src.at[inst], q_rcv.at[0, inst], 1, {"inst": inst, "tp": high}, 0).start()

    @pl.when(is_high)
    def _():
        for to in peers:
            remote(q_src.at[to], q_rcv.at[1, inst], 1, {"inst": to, "tp": tp}, 1).start()
            remote(sq_src, sq_rcv.at[inst], 0, {"inst": to, "tp": tp}, 5).start()
        q_rcv[1, inst] = q_src[inst]
        sq_rcv[inst] = sq_src[...]

    for g in range(4):

        @pl.when((inst != g) | is_low)
        def _():
            remote(kv_src.at[g], kv_rcv.at[core, inst], 2, {"inst": g, "tp": high}, 2 + core).start()

    @pl.when(is_low)
    def _():
        remote(wo_hbm, wo.at[0], 9, {"inst": inst, "tp": high}, 7).start()

    loads[6].wait()

    loads[4].wait()
    loads[5].wait()
    row = iota((16, 512), 0)
    shifted = iota((16, 512), 1) - ((row // 2) * 64 + lax.rem(row, 2) * 8)
    column = iota((1, 512), 1)

    def slot(s, targets):
        owner = owns[s]
        safe = jnp.maximum(owner, 0)
        target = jnp.where(owner >= 0, (safe // 8) * 16 + lax.rem(safe, 8), -1000)
        limit = jnp.where(owner >= 0, lens[safe] - pages[s] * 256, 0)
        sel[pl.ds(pl.multiple_of(16 * s, 16), 16), :] = (shifted == target).astype(F32).astype(BF16)
        bias[s] = jnp.where(iota((1, 256), 1) < limit, 0.0, NEG)
        member[s] = (iota((1, HD), 1) == owner).astype(jnp.int32)
        return jnp.where(column // 16 == s, target, targets)

    targets = lax.fori_loop(0, 32, slot, jnp.zeros((1, 512), jnp.int32), unroll=4)
    j = lax.rem(column, 16)
    targets = targets + (j // 2) * 64 + lax.rem(j, 2) * 8
    turned = lax.rem(iota((512, 512), 0) + 64 * lax.rem(z + 2, 8), 512)
    sel_t[...] = (turned == targets).astype(F32).astype(BF16)

    @pl.when(is_high)
    def _():
        loads[9].start()
        spot = iota((16, HD), 0)
        lane = iota((16, HD), 1)
        position = jnp.zeros((16, HD), jnp.int32)
        for k in range(8):
            position = jnp.where(lax.rem(spot, 8) == k, lens[8 * x + k], position)
        position = position + spot // 8
        index = lax.rem(lane, 64).astype(F32)
        angle = position.astype(F32) * jnp.exp(index * (-2.0 / HD * 13.122363377404328))
        cosine = jnp.cos(angle)
        sine = jnp.sin(angle) * jnp.where(lane < 64, -1.0, 1.0)
        arrived(sq_rcv.at[0:31], 5)
        total = jnp.sum(sq_rcv[...], axis=0)
        mine = jnp.where(lane == 16 * x + spot, total, 0.0)
        inverse = lax.rsqrt(jnp.sum(mine, axis=1, keepdims=True) / D + EPS)
        arrived(q_rcv.at[1, 0:31], 1)
        joined = jnp.sum(q_rcv[1].astype(F32), axis=0)
        q_all[inst] = rope(joined * inverse, cosine, sine).astype(BF16)
        for to in peers:
            remote(q_all.at[inst], q_all.at[inst], 10, {"inst": to, "tp": tp}, 4).start()
        arrived(q_rcv.at[0], 0)
        joined = jnp.sum(q_rcv[0].astype(F32), axis=0)
        q_low[...] = rope(joined * inverse, cosine, sine).astype(BF16)
        for to in peers:
            remote(q_low, q_all.at[inst], 3, {"inst": to, "tp": low}, 4).start()
        remote(q_low, q_all.at[inst], 3, {"inst": inst, "tp": low}, 4).start()

        @pl.when(z == 0)
        def _():
            kv_rcv[1, inst] = kv_src[x]
            arrived(kv_rcv.at[0], 2)
            arrived(kv_rcv.at[1, 0:31], 3)
            for c in range(2):
                both = jnp.sum(kv_rcv[c].astype(F32), axis=0)
                both = both * jnp.concatenate([inverse, inverse], axis=0)
                kv_new[c, 0:16, :] = rope(both[0:16], cosine, sine).astype(BF16)
                kv_new[c, 16:32, :] = both[16:32].astype(BF16)
            for k in range(1, 8):
                remote(kv_new, kv_new, 4, {"inst": 4 * k + x, "tp": tp}, 6).start()

    loads[7].wait()
    loads[8].wait()

    @pl.when(is_low)
    def _():
        arrived(q_all, 4)

    @pl.when(is_high)
    def _():
        arrived(q_all.at[0:31], 4)

    queries = jnp.dot(sel[...], q_all[...].reshape(512, HD), preferred_element_type=F32).astype(BF16)
    scores = lax.dot_general(
        queries.reshape(32, 16, HD), keys[...], (((2,), (2,)), ((0,), (0,))), preferred_element_type=F32
    )
    scores = scores * SCALE + bias[...]
    top = jnp.max(scores, axis=2, keepdims=True)
    weights = jnp.exp(scores - top)
    weight_sum = jnp.sum(weights, axis=2, keepdims=True)
    part = lax.dot_general(
        weights.astype(BF16), vals[...], (((2,), (1,)), ((0,), (0,))), preferred_element_type=F32
    )
    belongs = member[...] > 0
    top_req = jnp.max(jnp.where(belongs, top, NEG), axis=0)
    peak = jnp.max(jnp.where(belongs, top_req[None], NEG), axis=2, keepdims=True)
    factor = jnp.exp(top - peak)
    sum_req = jnp.sum(jnp.where(belongs, factor * weight_sum, 0.0), axis=0)
    stats = jnp.where(iota((16, HD), 1) < 32, top_req, pltpu.roll(sum_req, 32, 1))
    st_src[...] = stats.reshape(8, 2, HD)
    def send_stats(dz, dx):
        zo, xo = lax.rem(z + dz, 8), lax.rem(x + dx, 4)
        to = {"inst": zo * 4 + xo, "tp": high}
        remote(st_src.at[zo], st_rcv.at[core, inst], 5, to, 8 + core).start()

    for dz, dx in offsets[:31]:
        send_stats(dz, dx)
    part = (part * factor).reshape(512, HD)
    high_part = part.astype(BF16)
    low_part = (part - high_part.astype(F32)).astype(BF16)
    parts = jnp.concatenate([high_part, low_part], axis=1)

    def send_part(dz, dx):
        zo, xo = lax.rem(z + dz, 8), lax.rem(x + dx, 4)
        to = {"inst": zo * 4 + xo, "tp": high}
        held = acc_src.at[4 * ((dz - 2) % 8) + xo]
        remote(held, acc_rcv.at[core, inst], 6, to, 10 + core).start()

    for half in range(2):
        rows = slice(256 * half, 256 * half + 256)
        both = jnp.dot(sel_t[rows, :], parts, preferred_element_type=F32)
        both = (both[:, :HD] + both[:, HD:]).astype(BF16)
        acc_src[16 * half : 16 * half + 16] = both.reshape(16, 16, HD)
        for dz, dx in offsets:
            if ((dz - 2) % 8 >= 4) == half:
                send_part(dz, dx)

    @pl.when(is_low)
    def _():
        send_part(0, 0)
        send_stats(0, 0)

    @pl.when(is_high)
    def _():
        acc_rcv[1, inst] = acc_src[24 + x]
        st_rcv[1, inst] = st_src[z]

        @pl.when(z > 0)
        def _():
            arrived(kv_new, 6)

        row = iota((16, 16), 0)
        key = iota((16, 16), 1)
        seen = (lax.rem(row, 8) == lax.rem(key, 8)) & (key // 8 <= row // 8)
        fresh_tops, fresh_sums, fresh_outs = [], [], []
        for c in range(2):
            query = q_all[inst] if c else q_low[...]
            fresh = lax.dot_general(
                query, kv_new[c, 0:16, :], (((1,), (1,)), ((), ())), preferred_element_type=F32
            ) * SCALE
            fresh = jnp.where(seen, fresh, NEG)
            fresh_top = jnp.max(fresh, axis=1, keepdims=True)
            weights = jnp.where(seen, jnp.exp(fresh - fresh_top), 0.0)
            fresh_tops.append(fresh_top)
            fresh_sums.append(jnp.sum(weights, axis=1, keepdims=True))
            fresh_outs.append(
                jnp.dot(weights.astype(BF16), kv_new[c, 16:32, :], preferred_element_type=F32)
            )

        for c in (1, 0):
            arrived(st_rcv.at[1, 0:31] if c else st_rcv.at[0], 8 + c)
            stats = jnp.concatenate([st_rcv[c, :, 0, :], st_rcv[c, :, 1, :]], axis=0)
            stats = pltpu.roll(stats, lax.rem(HD - 8 * x, HD), 1).T
            tops, sums = stats[0:8], stats[32:40]
            scales, fresh_scales, totals = [], [], []
            for t in range(2):
                first = fresh_tops[c][8 * t : 8 * t + 8]
                held = tops[:, 32 * t : 32 * t + 32]
                peak = jnp.maximum(jnp.max(held, axis=1, keepdims=True), first)
                scale = jnp.exp(held - peak)
                fresh_scale = jnp.exp(first - peak)
                total = jnp.sum(scale * sums[:, 32 * t : 32 * t + 32], axis=1, keepdims=True)
                totals.append(total + fresh_scale * fresh_sums[c][8 * t : 8 * t + 8])
                scales.append(scale)
                fresh_scales.append(fresh_scale)
            scale = jnp.concatenate(scales, axis=0)
            arrived(acc_rcv.at[1, 0:31] if c else acc_rcv.at[0], 10 + c)
            out = jnp.concatenate(fresh_scales, axis=0) * fresh_outs[c]
            for d in range(N_INST):
                out = out + scale[:, d : d + 1] * acc_rcv[c, d].astype(F32)
            att_all[x, z, c] = (out / jnp.concatenate(totals, axis=0)).astype(BF16)

        for k in range(N_INST - 1):
            to = k + (k >= inst).astype(jnp.int32)
            group = lax.rem(x - lax.rem(to, 4) + 4, 4)
            remote(att_all.at[x, z], att_all.at[x, z], 7, {"inst": to, "tp": tp}, 12 + group).start()

        loads[9].wait()
        arrived(wo.at[0], 7)
        for k in (0, 1, 3, 2):
            g = lax.rem(x + k, 4)
            arrived(att_all.at[g] if k else att_all.at[g, 0:7], 12 + k)
            attention = jnp.concatenate([att_all[g, h, c] for c in range(2) for h in range(8)], axis=1)
            projected = jnp.dot(attention, wo[...].reshape(2048, 256), preferred_element_type=F32)
            tp_all[y, g] = projected.astype(BF16)
            for to in tp_peers:
                remote(tp_all.at[y, g], tp_all.at[y, g], 8, {"inst": inst, "tp": to}, 16 + k).start()

    for k in (0, 1, 3, 2):
        g = lax.rem(x + k, 4)

        @pl.when(is_low)
        def _():
            arrived(tp_all.at[:, g], 16 + k)

        @pl.when(is_high)
        def _():
            arrived(tp_all.at[0:3, g], 16 + k)

        mixed = tp_all[0, g].astype(F32)
        for d in range(1, 4):
            mixed = mixed + tp_all[d, g].astype(F32)
        for t in range(2):
            for c in range(2):
                held = mixed[8 * t : 8 * t + 8, HD * c : HD * c + HD]
                out_ref[c, g, pl.ds(t, 8, stride=2), :] = held

    @pl.when(is_low)
    def _():
        departed(q_rcv.at[0], 1)
        departed(kv_src, 2)
        departed(st_rcv.at[0], 5)
        departed(acc_rcv.at[0], 6)
        departed(wo.at[0], 9)

    @pl.when(is_high)
    def _():
        departed(sq_rcv.at[0:31], 0)
        departed(q_rcv.at[1, 0:31], 1)

        @pl.when(z == 0)
        def _():
            departed(kv_src.at[0:3], 2)
            departed(kv_rcv.at[0, 0:14], 4)

        @pl.when(z > 0)
        def _():
            departed(kv_src, 2)

        departed(q_rcv.at[0], 3)
        departed(q_rcv.at[1, 0:31], 10)
        departed(st_rcv.at[1, 0:31], 5)
        departed(acc_rcv.at[1, 0:31], 6)
        departed(acc_rcv.at[:, 0:31], 7)
        departed(wo.at[0, 0:448], 8)


def on_device(*arrays):
    hbm = pl.BlockSpec(memory_space=pltpu.HBM)
    vmem = pl.BlockSpec(memory_space=pltpu.VMEM)
    mixed = pl.pallas_call(
        kernel,
        out_shape=pltpu.VMEM((2, 4, 16, HD), F32),
        in_specs=[hbm] * 10,
        out_specs=vmem,
        scratch_shapes=[
            pltpu.VMEM((64, 256), BF16),
            pltpu.VMEM((2, 64, HD), F32),
            pltpu.VMEM((256,), BF16),
            pltpu.VMEM((256, 1024), BF16),
            pltpu.VMEM((256, 256), BF16),
            pltpu.VMEM((2, 1024, 256), BF16),
            pltpu.VMEM((32, 256, HD), BF16),
            pltpu.VMEM((32, 256, HD), BF16),
            pltpu.SMEM((32,), jnp.int32),
            pltpu.SMEM((32,), jnp.int32),
            pltpu.SMEM((32,), jnp.int32),
            pltpu.VMEM((N_INST, 16, HD), BF16),
            pltpu.VMEM((2, N_INST, 16, HD), BF16),
            pltpu.VMEM((4, 32, HD), BF16),
            pltpu.VMEM((2, N_INST, 32, HD), BF16),
            pltpu.VMEM((1, HD), F32),
            pltpu.VMEM((N_INST, 1, HD), F32),
            pltpu.VMEM((N_INST, 16, HD), BF16),
            pltpu.VMEM((16, HD), BF16),
            pltpu.VMEM((2, 32, HD), BF16),
            pltpu.VMEM((512, 512), BF16),
            pltpu.VMEM((512, 512), BF16),
            pltpu.VMEM((32, 1, 256), F32),
            pltpu.VMEM((32, 1, HD), jnp.int32),
            pltpu.VMEM((N_INST, 16, HD), BF16),
            pltpu.VMEM((2, N_INST, 16, HD), BF16),
            pltpu.VMEM((8, 2, HD), F32),
            pltpu.VMEM((2, N_INST, 2, HD), F32),
            pltpu.VMEM((4, 8, 2, 16, HD), BF16),
            pltpu.VMEM((4, 4, 16, 256), BF16),
            pltpu.SemaphoreType.DMA((11,)),
            pltpu.SemaphoreType.DMA((11,)),
            pltpu.SemaphoreType.DMA((20,)),
        ],
        compiler_params=pltpu.CompilerParams(
            collective_id=0, has_side_effects=True, vmem_limit_bytes=48 * 1024 * 1024
        ),
        name="paged_attention",
    )(*(pltpu.with_memory_space_constraint(a, pltpu.HBM) for a in arrays))
    return mixed.transpose(1, 2, 0, 3).reshape(64, 256).astype(BF16)


def solution(mesh):
    return jax.shard_map(
        on_device,
        mesh=mesh,
        in_specs=(
            P(None, "inst"),
            P("inst"),
            P("inst", "tp"),
            P("inst", "tp"),
            P("inst", "tp"),
            P("tp", "inst"),
            P(None, "inst", None, "tp"),
            P(),
            P("inst"),
            P("inst"),
        ),
        out_specs=P(None, "inst"),
        check_vma=False,
    )
```

```python
import functools

import jax
import jax.numpy as jnp
from jax import lax
from jax.experimental import pallas as pl
from jax.experimental.pallas import tpu as pltpu
from jax.sharding import PartitionSpec as P

D = 8192
HD = 128
NEG = -1e30
EPS = 1e-05
THETA = 500000.0
SCALE = HD ** -0.5
N_INST = 32
N_TP = 8
MESH = pl.DeviceIdType.MESH
F32 = jnp.float32
BF16 = jnp.bfloat16


def iota(shape, dim):
    return lax.broadcasted_iota(jnp.int32, shape, dim)


def far_first():
    offsets = [(dz, dx) for dz in range(8) for dx in range(4) if dz or dx]
    return sorted(offsets, key=lambda o: -min(o[0], 8 - o[0]) - min(o[1], 4 - o[1]))


def rope(rows, cosine, sine):
    return rows * cosine + pltpu.roll(rows, 64, 1) * sine


def kernel(
    hid_hbm, gain_hbm, wq_hbm, wk_hbm, wv_hbm, wo_hbm, kv_hbm, len_hbm, own_hbm, page_hbm,
    out_ref,
    hid, hid32, gain, wq, wkv, wo, keys, vals, lens, owns, pages,
    q_src, q_rcv, kv_src, kv_rcv, sq_src, sq_rcv, q_all, q_low, kv_new,
    sel, sel_t, bias, member, acc_src, acc_rcv, st_src, st_rcv, att_all, tp_all,
    local_sem, send_sem, recv_sem,
):
    inst = lax.axis_index("inst")
    tp = lax.axis_index("tp")
    z, x = inst // 4, lax.rem(inst, 4)
    core, y = lax.rem(tp, 2), tp // 2
    low = tp - core
    high = low + 1
    is_low, is_high = core == 0, core == 1
    offsets = far_first()
    peers = [lax.rem(z + dz, 8) * 4 + lax.rem(x + dx, 4) for dz, dx in offsets]
    tp_peers = [lax.rem(tp + k, N_TP) for k in (4, 5, 3, 2, 6, 1, 7)]

    def local(i, src, dst):
        return pltpu.make_async_copy(src, dst, local_sem.at[i])

    loads = [
        local(0, hid_hbm, hid),
        local(1, wq_hbm, wq),
        local(2, wk_hbm, wkv.at[:, :HD]),
        local(3, wv_hbm, wkv.at[:, HD:]),
        local(4, own_hbm, owns),
        local(5, page_hbm, pages),
        local(6, len_hbm, lens),
        local(7, kv_hbm.at[0], keys),
        local(8, kv_hbm.at[1], vals),
        local(9, wo_hbm, wo.at[1]),
        local(10, gain_hbm, gain),
    ]
    barrier = pltpu.get_barrier_semaphore()

    def greet(to):
        pl.semaphore_signal(barrier, inc=1, device_id=to, device_id_type=MESH)

    @pl.when(is_high)
    def _():
        for to in peers:
            greet({"inst": to, "tp": tp})
            greet({"inst": to, "tp": low})

    for to in tp_peers:
        greet({"inst": inst, "tp": to})
    for load in [loads[0], loads[10]] + loads[1:9]:
        load.start()

    def remote(src, dst, i, to, into):
        return pltpu.make_async_remote_copy(
            src_ref=src, dst_ref=dst, send_sem=send_sem.at[i], recv_sem=recv_sem.at[into],
            device_id=to, device_id_type=MESH,
        )

    def arrived(ref, i):
        pltpu.make_async_copy(ref, ref, recv_sem.at[i]).wait()

    def departed(ref, i):
        pltpu.make_async_copy(ref, ref, send_sem.at[i]).wait()

    loads[0].wait()
    for c in range(2):
        hid32[c] = hid[:, HD * c : HD * c + HD].astype(F32)
    rows = jnp.concatenate(
        [
            jnp.concatenate(
                [hid32[c, pl.ds(16 * g + t, 8, stride=2), :] for g in range(4) for t in range(2)], axis=0
            )
            for c in range(2)
        ],
        axis=1,
    )
    squares = jnp.sum(rows * rows, axis=1, keepdims=True)
    spread = jnp.where(iota((64, HD), 0) == iota((64, HD), 1), squares, 0.0)
    sq_src[...] = jnp.sum(spread, axis=0, keepdims=True)
    loads[10].wait()
    normed = (rows * gain[...].astype(F32).reshape(1, 256)).astype(BF16)
    loads[1].wait()
    raw = jnp.dot(normed, wq[...], preferred_element_type=F32).astype(BF16)
    for h in range(8):
        for g in range(4):
            q_src[4 * h + g] = raw[16 * g : 16 * g + 16, HD * h : HD * h + HD]
    loads[2].wait()
    loads[3].wait()
    raw = jnp.dot(normed, wkv[...], preferred_element_type=F32).astype(BF16)
    for g in range(4):
        for k in range(2):
            kv_src[g, 16 * k : 16 * k + 16, :] = raw[16 * g : 16 * g + 16, HD * k : HD * k + HD]

    pl.semaphore_wait(barrier, N_INST - 1 + N_TP - 1)

    @pl.when(is_low)
    def _():
        for to in peers:
            remote(q_src.at[to], q_rcv.at[0, inst], 1, {"inst": to, "tp": high}, 0).start()
        remote(q_src.at[inst], q_rcv.at[0, inst], 1, {"inst": inst, "tp": high}, 0).start()

    @pl.when(is_high)
    def _():
        for to in peers:
            remote(q_src.at[to], q_rcv.at[1, inst], 1, {"inst": to, "tp": tp}, 1).start()
            remote(sq_src, sq_rcv.at[inst], 0, {"inst": to, "tp": tp}, 5).start()
        q_rcv[1, inst] = q_src[inst]
        sq_rcv[inst] = sq_src[...]

    for g in range(4):

        @pl.when((inst != g) | is_low)
        def _():
            remote(kv_src.at[g], kv_rcv.at[core, inst], 2, {"inst": g, "tp": high}, 2 + core).start()

    @pl.when(is_low)
    def _():
        remote(wo_hbm, wo.at[0], 9, {"inst": inst, "tp": high}, 7).start()

    loads[6].wait()

    loads[4].wait()
    loads[5].wait()
    row = iota((16, 512), 0)
    shifted = iota((16, 512), 1) - ((row // 2) * 64 + lax.rem(row, 2) * 8)
    column = iota((1, 512), 1)

    def slot(s, targets):
        owner = owns[s]
        safe = jnp.maximum(owner, 0)
        target = jnp.where(owner >= 0, (safe // 8) * 16 + lax.rem(safe, 8), -1000)
        limit = jnp.where(owner >= 0, lens[safe] - pages[s] * 256, 0)
        sel[pl.ds(pl.multiple_of(16 * s, 16), 16), :] = (shifted == target).astype(F32).astype(BF16)
        bias[s] = jnp.where(iota((1, 256), 1) < limit, 0.0, NEG)
        member[s] = (iota((1, HD), 1) == owner).astype(jnp.int32)
        return jnp.where(column // 16 == s, target, targets)

    targets = lax.fori_loop(0, 32, slot, jnp.zeros((1, 512), jnp.int32), unroll=4)
    j = lax.rem(column, 16)
    targets = targets + (j // 2) * 64 + lax.rem(j, 2) * 8
    turned = lax.rem(iota((512, 512), 0) + 64 * lax.rem(z + 2, 8), 512)
    sel_t[...] = (turned == targets).astype(F32).astype(BF16)

    @pl.when(is_high)
    def _():
        loads[9].start()
        spot = iota((16, HD), 0)
        lane = iota((16, HD), 1)
        position = jnp.zeros((16, HD), jnp.int32)
        for k in range(8):
            position = jnp.where(lax.rem(spot, 8) == k, lens[8 * x + k], position)
        position = position + spot // 8
        index = lax.rem(lane, 64).astype(F32)
        angle = position.astype(F32) * jnp.exp(index * (-2.0 / HD * 13.122363377404328))
        cosine = jnp.cos(angle)
        sine = jnp.sin(angle) * jnp.where(lane < 64, -1.0, 1.0)
        arrived(sq_rcv.at[0:31], 5)
        total = jnp.sum(sq_rcv[...], axis=0)
        mine = jnp.where(lane == 16 * x + spot, total, 0.0)
        inverse = lax.rsqrt(jnp.sum(mine, axis=1, keepdims=True) / D + EPS)
        arrived(q_rcv.at[1, 0:31], 1)
        joined = jnp.sum(q_rcv[1].astype(F32), axis=0)
        q_all[inst] = rope(joined * inverse, cosine, sine).astype(BF16)
        for to in peers:
            remote(q_all.at[inst], q_all.at[inst], 10, {"inst": to, "tp": tp}, 4).start()
        arrived(q_rcv.at[0], 0)
        joined = jnp.sum(q_rcv[0].astype(F32), axis=0)
        q_low[...] = rope(joined * inverse, cosine, sine).astype(BF16)
        for to in peers:
            remote(q_low, q_all.at[inst], 3, {"inst": to, "tp": low}, 4).start()
        remote(q_low, q_all.at[inst], 3, {"inst": inst, "tp": low}, 4).start()

        @pl.when(z == 0)
        def _():
            kv_rcv[1, inst] = kv_src[x]
            arrived(kv_rcv.at[0], 2)
            arrived(kv_rcv.at[1, 0:31], 3)
            for c in range(2):
                both = jnp.sum(kv_rcv[c].astype(F32), axis=0)
                both = both * jnp.concatenate([inverse, inverse], axis=0)
                kv_new[c, 0:16, :] = rope(both[0:16], cosine, sine).astype(BF16)
                kv_new[c, 16:32, :] = both[16:32].astype(BF16)
            for k in range(1, 8):
                remote(kv_new, kv_new, 4, {"inst": 4 * k + x, "tp": tp}, 6).start()

    loads[7].wait()
    loads[8].wait()

    @pl.when(is_low)
    def _():
        arrived(q_all, 4)

    @pl.when(is_high)
    def _():
        arrived(q_all.at[0:31], 4)

    queries = jnp.dot(sel[...], q_all[...].reshape(512, HD), preferred_element_type=F32).astype(BF16)
    scores = lax.dot_general(
        queries.reshape(32, 16, HD), keys[...], (((2,), (2,)), ((0,), (0,))), preferred_element_type=F32
    )
    scores = scores * SCALE + bias[...]
    top = jnp.max(scores, axis=2, keepdims=True)
    weights = jnp.exp(scores - top)
    weight_sum = jnp.sum(weights, axis=2, keepdims=True)
    part = lax.dot_general(
        weights.astype(BF16), vals[...], (((2,), (1,)), ((0,), (0,))), preferred_element_type=F32
    )
    belongs = member[...] > 0
    top_req = jnp.max(jnp.where(belongs, top, NEG), axis=0)
    peak = jnp.max(jnp.where(belongs, top_req[None], NEG), axis=2, keepdims=True)
    factor = jnp.exp(top - peak)
    sum_req = jnp.sum(jnp.where(belongs, factor * weight_sum, 0.0), axis=0)
    stats = jnp.where(iota((16, HD), 1) < 32, top_req, pltpu.roll(sum_req, 32, 1))
    st_src[...] = stats.reshape(8, 2, HD)
    def send_stats(dz, dx):
        zo, xo = lax.rem(z + dz, 8), lax.rem(x + dx, 4)
        to = {"inst": zo * 4 + xo, "tp": high}
        remote(st_src.at[zo], st_rcv.at[core, inst], 5, to, 8 + core).start()

    for dz, dx in offsets[:31]:
        send_stats(dz, dx)
    part = (part * factor).reshape(512, HD)
    parts = part.astype(BF16)

    def send_part(dz, dx):
        zo, xo = lax.rem(z + dz, 8), lax.rem(x + dx, 4)
        to = {"inst": zo * 4 + xo, "tp": high}
        held = acc_src.at[4 * ((dz - 2) % 8) + xo]
        remote(held, acc_rcv.at[core, inst], 6, to, 10 + core).start()

    for half in range(2):
        rows = slice(256 * half, 256 * half + 256)
        both = jnp.dot(sel_t[rows, :], parts, preferred_element_type=F32)
        both = both.astype(BF16)
        acc_src[16 * half : 16 * half + 16] = both.reshape(16, 16, HD)
        for dz, dx in offsets:
            if ((dz - 2) % 8 >= 4) == half:
                send_part(dz, dx)

    @pl.when(is_low)
    def _():
        send_part(0, 0)
        send_stats(0, 0)

    @pl.when(is_high)
    def _():
        acc_rcv[1, inst] = acc_src[24 + x]
        st_rcv[1, inst] = st_src[z]

        @pl.when(z > 0)
        def _():
            arrived(kv_new, 6)

        row = iota((16, 16), 0)
        key = iota((16, 16), 1)
        seen = (lax.rem(row, 8) == lax.rem(key, 8)) & (key // 8 <= row // 8)
        fresh_tops, fresh_sums, fresh_outs = [], [], []
        for c in range(2):
            query = q_all[inst] if c else q_low[...]
            fresh = lax.dot_general(
                query, kv_new[c, 0:16, :], (((1,), (1,)), ((), ())), preferred_element_type=F32
            ) * SCALE
            fresh = jnp.where(seen, fresh, NEG)
            fresh_top = jnp.max(fresh, axis=1, keepdims=True)
            weights = jnp.where(seen, jnp.exp(fresh - fresh_top), 0.0)
            fresh_tops.append(fresh_top)
            fresh_sums.append(jnp.sum(weights, axis=1, keepdims=True))
            fresh_outs.append(
                jnp.dot(weights.astype(BF16), kv_new[c, 16:32, :], preferred_element_type=F32)
            )

        for c in (1, 0):
            arrived(st_rcv.at[1, 0:31] if c else st_rcv.at[0], 8 + c)
            stats = jnp.concatenate([st_rcv[c, :, 0, :], st_rcv[c, :, 1, :]], axis=0)
            stats = pltpu.roll(stats, lax.rem(HD - 8 * x, HD), 1).T
            tops, sums = stats[0:8], stats[32:40]
            scales, fresh_scales, totals = [], [], []
            for t in range(2):
                first = fresh_tops[c][8 * t : 8 * t + 8]
                held = tops[:, 32 * t : 32 * t + 32]
                peak = jnp.maximum(jnp.max(held, axis=1, keepdims=True), first)
                scale = jnp.exp(held - peak)
                fresh_scale = jnp.exp(first - peak)
                total = jnp.sum(scale * sums[:, 32 * t : 32 * t + 32], axis=1, keepdims=True)
                totals.append(total + fresh_scale * fresh_sums[c][8 * t : 8 * t + 8])
                scales.append(scale)
                fresh_scales.append(fresh_scale)
            scale = jnp.concatenate(scales, axis=0)
            arrived(acc_rcv.at[1, 0:31] if c else acc_rcv.at[0], 10 + c)
            out = jnp.concatenate(fresh_scales, axis=0) * fresh_outs[c]
            for d in range(N_INST):
                out = out + scale[:, d : d + 1] * acc_rcv[c, d].astype(F32)
            att_all[x, z, c] = (out / jnp.concatenate(totals, axis=0)).astype(BF16)

        for k in range(N_INST - 1):
            to = k + (k >= inst).astype(jnp.int32)
            group = lax.rem(x - lax.rem(to, 4) + 4, 4)
            remote(att_all.at[x, z], att_all.at[x, z], 7, {"inst": to, "tp": tp}, 12 + group).start()

        loads[9].wait()
        arrived(wo.at[0], 7)
        for k in (0, 1, 3, 2):
            g = lax.rem(x + k, 4)
            arrived(att_all.at[g] if k else att_all.at[g, 0:7], 12 + k)
            attention = jnp.concatenate([att_all[g, h, c] for c in range(2) for h in range(8)], axis=1)
            projected = jnp.dot(attention, wo[...].reshape(2048, 256), preferred_element_type=F32)
            tp_all[y, g] = projected.astype(BF16)
            for to in tp_peers:
                remote(tp_all.at[y, g], tp_all.at[y, g], 8, {"inst": inst, "tp": to}, 16 + k).start()

    for k in (0, 1, 3, 2):
        g = lax.rem(x + k, 4)

        @pl.when(is_low)
        def _():
            arrived(tp_all.at[:, g], 16 + k)

        @pl.when(is_high)
        def _():
            arrived(tp_all.at[0:3, g], 16 + k)

        mixed = tp_all[0, g].astype(F32)
        for d in range(1, 4):
            mixed = mixed + tp_all[d, g].astype(F32)
        for t in range(2):
            for c in range(2):
                held = mixed[8 * t : 8 * t + 8, HD * c : HD * c + HD]
                out_ref[c, g, pl.ds(t, 8, stride=2), :] = held

    @pl.when(is_low)
    def _():
        departed(q_rcv.at[0], 1)
        departed(kv_src, 2)
        departed(st_rcv.at[0], 5)
        departed(acc_rcv.at[0], 6)
        departed(wo.at[0], 9)

    @pl.when(is_high)
    def _():
        departed(sq_rcv.at[0:31], 0)
        departed(q_rcv.at[1, 0:31], 1)

        @pl.when(z == 0)
        def _():
            departed(kv_src.at[0:3], 2)
            departed(kv_rcv.at[0, 0:14], 4)

        @pl.when(z > 0)
        def _():
            departed(kv_src, 2)

        departed(q_rcv.at[0], 3)
        departed(q_rcv.at[1, 0:31], 10)
        departed(st_rcv.at[1, 0:31], 5)
        departed(acc_rcv.at[1, 0:31], 6)
        departed(acc_rcv.at[:, 0:31], 7)
        departed(wo.at[0, 0:448], 8)


def on_device(*arrays):
    hbm = pl.BlockSpec(memory_space=pltpu.HBM)
    vmem = pl.BlockSpec(memory_space=pltpu.VMEM)
    mixed = pl.pallas_call(
        kernel,
        out_shape=pltpu.VMEM((2, 4, 16, HD), F32),
        in_specs=[hbm] * 10,
        out_specs=vmem,
        scratch_shapes=[
            pltpu.VMEM((64, 256), BF16),
            pltpu.VMEM((2, 64, HD), F32),
            pltpu.VMEM((256,), BF16),
            pltpu.VMEM((256, 1024), BF16),
            pltpu.VMEM((256, 256), BF16),
            pltpu.VMEM((2, 1024, 256), BF16),
            pltpu.VMEM((32, 256, HD), BF16),
            pltpu.VMEM((32, 256, HD), BF16),
            pltpu.SMEM((32,), jnp.int32),
            pltpu.SMEM((32,), jnp.int32),
            pltpu.SMEM((32,), jnp.int32),
            pltpu.VMEM((N_INST, 16, HD), BF16),
            pltpu.VMEM((2, N_INST, 16, HD), BF16),
            pltpu.VMEM((4, 32, HD), BF16),
            pltpu.VMEM((2, N_INST, 32, HD), BF16),
            pltpu.VMEM((1, HD), F32),
            pltpu.VMEM((N_INST, 1, HD), F32),
            pltpu.VMEM((N_INST, 16, HD), BF16),
            pltpu.VMEM((16, HD), BF16),
            pltpu.VMEM((2, 32, HD), BF16),
            pltpu.VMEM((512, 512), BF16),
            pltpu.VMEM((512, 512), BF16),
            pltpu.VMEM((32, 1, 256), F32),
            pltpu.VMEM((32, 1, HD), jnp.int32),
            pltpu.VMEM((N_INST, 16, HD), BF16),
            pltpu.VMEM((2, N_INST, 16, HD), BF16),
            pltpu.VMEM((8, 2, HD), F32),
            pltpu.VMEM((2, N_INST, 2, HD), F32),
            pltpu.VMEM((4, 8, 2, 16, HD), BF16),
            pltpu.VMEM((4, 4, 16, 256), BF16),
            pltpu.SemaphoreType.DMA((11,)),
            pltpu.SemaphoreType.DMA((11,)),
            pltpu.SemaphoreType.DMA((20,)),
        ],
        compiler_params=pltpu.CompilerParams(
            collective_id=0, has_side_effects=True, vmem_limit_bytes=48 * 1024 * 1024
        ),
        name="paged_attention",
    )(*(pltpu.with_memory_space_constraint(a, pltpu.HBM) for a in arrays))
    return mixed.transpose(1, 2, 0, 3).reshape(64, 256).astype(BF16)


def solution(mesh):
    return jax.shard_map(
        on_device,
        mesh=mesh,
        in_specs=(
            P(None, "inst"),
            P("inst"),
            P("inst", "tp"),
            P("inst", "tp"),
            P("inst", "tp"),
            P("tp", "inst"),
            P(None, "inst", None, "tp"),
            P(),
            P("inst"),
            P("inst"),
        ),
        out_specs=P(None, "inst"),
        check_vma=False,
    )
```
